256 devices in a mesh: role: 2 (over x_lo), grp: 16 (over x_hi, z), tp: 8 (over y, core).
Axes of the slice: x: 4 (x_hi: 2, x_lo: 2; x = x_hi * 2 + x_lo), y: 4, z: 8, core: 2. Of those that a mesh axis runs over, the one named last changes fastest.
Arguments:
- prompt_states: bfloat16 [2, 16, 512, 5120], P('role', 'grp', 'tp'), may hold values from -6 to 6
- new_states: bfloat16 [2, 256, 2, 5120], P('role', 'grp'), may hold values from -6 to 6
- answer_cache: bfloat16 [2, 256, 128, 2048], P('role', 'grp', None, 'tp'), may hold values from -6 to 6
- attn_gain: float32 [5120], replicated, may hold values from 0.1 to 1.9
- w_query: bfloat16 [5120, 3072], P(None, 'tp')
- key_weight: bfloat16 [5120, 1024], P(None, 'tp')
- value_weight: bfloat16 [5120, 1024], P(None, 'tp'), may hold values from -0.078125 to 0.078125
- w_out: bfloat16 [3072, 5120], P('tp'), may hold values from -0.15625 to 0.15625
- prompt_of: int32 [2, 256], P('role'), may hold values from 0 to 15, as said below
- suffix_len: int32 [2, 256], P('role', 'grp'), may hold values from 1 to 128, as said below
Outputs:
- prefill_out: bfloat16 [2, 16, 512, 5120], P('role', 'grp', 'tp')
- decode_out: float32 [2, 256, 2, 5120], P('role', 'grp')
The draws below stay inside these ranges and needn't reach their ends.
Inputs may be any that keep to these rules, and one draw needn't show every extreme that they name: `prompt_of`: in each half every prompt index 0 to 15 appears exactly 16 times. `suffix_len`: each aligned block of 16 samples holds one sample of length 128.
All inputs are finite; a program needn't handle non-finite values.
Results may differ from the reference program's by a relative error of at most 0.017.
Values may be sent and summed in bfloat16 or wider, within the bound.
No kernel may reach another device: no remote copies, remote signals or barrier semaphores. Data moves between devices by JAX's collectives and lax.ppermute only.
A program may use at most 128 MiB of HBM per device.

```python
import jax
import jax.numpy as jnp
from jax import lax

MODEL_WIDTH = 5120
QUERY_HEADS = 24
KEY_VALUE_HEADS = 8
HEAD_WIDTH = 128
S = 16
PROMPT_LENGTH = 512
SUFFIX_LENGTH = 128
SAMPLE_COUNT = 256
N_GRP = 16
N_TP = 8


def shared_query(key):
    return jax.random.normal(key, (MODEL_WIDTH, QUERY_HEADS * HEAD_WIDTH), jnp.float32) * MODEL_WIDTH ** (-0.5)


def draw_w_query(key, part):
    base_offset = shared_query(key)
    return base_offset.astype(jnp.bfloat16)


def draw_key_weight(key, part):
    key = jax.random.fold_in(key, 5)
    random_noise = jax.random.normal(key, (MODEL_WIDTH, KEY_VALUE_HEADS * HEAD_WIDTH), jnp.float32) * MODEL_WIDTH ** (-0.5)
    result = random_noise
    return result.astype(jnp.bfloat16)


def draw_prompt_of(key, part):
    key = jax.random.fold_in(key, 11)
    base_offset = jnp.repeat(jnp.arange(N_GRP, dtype=jnp.int32), S)
    first = jax.random.permutation(jax.random.fold_in(key, 1), base_offset)
    second = jax.random.permutation(jax.random.fold_in(key, 2), base_offset)
    return jnp.stack([first, second], axis=0).astype(jnp.int32)


def draw_suffix_len(key, part):
    key = jax.random.fold_in(key, 13)
    key_len, key_slot = jax.random.split(key)
    lengths = jax.random.randint(key_len, (2, N_GRP, S), 1, SUFFIX_LENGTH + 1, dtype=jnp.int32)
    chosen = jax.random.randint(key_slot, (2, N_GRP, 1), 0, S, dtype=jnp.int32)
    lengths = jnp.where(jnp.arange(S, dtype=jnp.int32) == chosen, SUFFIX_LENGTH, lengths)
    return lengths.reshape(2, N_GRP * S).astype(jnp.int32)


def with_spikes(values, stream_key, source, target, blocks, factor):
    owner, partner = [(jnp.arange(values.shape[position]) // (values.shape[position] // blocks)).reshape([-1 if axis == position else 1 for axis in range(values.ndim)]) for position in (source, target)]
    chosen = jax.random.permutation(stream_key, blocks)[partner]
    strong = (owner == chosen) | (owner == (partner + blocks // 2) % blocks)
    return jnp.where(strong, factor * values, values)


def level_of(key, dims, cuts, low, largest):
    gain, own = 1.0, jax.random.fold_in(key, 6)
    for position, shards_of in cuts:
        draws = jnp.exp(jax.random.uniform(jax.random.fold_in(own, position), (shards_of,), jnp.float32, low / len(cuts), largest / len(cuts)))
        gain = gain * jnp.repeat(draws, dims[position] // shards_of).reshape([-1 if axis == position else 1 for axis in range(len(dims))])
    return gain


def bell_draw(stream_key, shape, spread, reach, cuts=(), kind=jnp.bfloat16):
    factor_of = level_of(stream_key, shape, cuts, -0.22, 0.18) if cuts else 1.0
    values = jax.random.normal(stream_key, shape, jnp.float32) * spread * factor_of
    return jnp.minimum(jnp.maximum(values, -reach), reach).astype(kind)


def gaussian_with(stream_key, extent, scale, bound, cuts, heavy, kind=jnp.bfloat16):
    values = scale * jax.random.normal(stream_key, extent, jnp.float32)
    if cuts:
        values = values * level_of(stream_key, extent, cuts, -0.22, 0.18)
    return jnp.clip(with_spikes(values, jax.random.fold_in(stream_key, 3), *heavy), -bound, bound).astype(kind)


def setup_inputs(seed: int = 0) -> dict:
    key_list = jax.random.split(jax.random.key(seed), 11)
    return {
        "prompt_states": bell_draw(key_list[0], (2, N_GRP, PROMPT_LENGTH, MODEL_WIDTH), 1.0, 6.0, ((0, 2), (1, 16), (2, 8))),
        "new_states": bell_draw(key_list[1], (2, SAMPLE_COUNT, 2, MODEL_WIDTH), 1.0, 6.0, ((0, 2), (1, 16))),
        "answer_cache": bell_draw(key_list[2], (2, SAMPLE_COUNT, SUFFIX_LENGTH, KEY_VALUE_HEADS * 2 * HEAD_WIDTH), 1.0, 6.0, ((0, 2), (1, 16), (3, 8))),
        "attn_gain": jnp.clip(1.0 + 0.18 * jax.random.normal(key_list[3], (MODEL_WIDTH,), jnp.float32), 0.1, 1.9),
        "w_query": draw_w_query(jax.random.fold_in(key_list[10], 71), 0),
        "key_weight": draw_key_weight(jax.random.fold_in(key_list[10], 71), 0),
        "value_weight": bell_draw(key_list[6], (MODEL_WIDTH, KEY_VALUE_HEADS * HEAD_WIDTH), MODEL_WIDTH ** -0.5, 0.078125, ((1, 8),)),
        "w_out": gaussian_with(key_list[7], (QUERY_HEADS * HEAD_WIDTH, MODEL_WIDTH), (QUERY_HEADS * HEAD_WIDTH) ** -0.5, 0.15625, ((0, 8),), (0, 1, 8, 2.0)),
        "prompt_of": draw_prompt_of(jax.random.fold_in(key_list[10], 71), 0),
        "suffix_len": draw_suffix_len(jax.random.fold_in(key_list[10], 71), 0),
    }


EPSILON = 1e-06
ROPE_BASE = 1000000.0

def normalize(entries, scales):
    wide = entries.astype(jnp.float32)
    factor = lax.rsqrt(lax.optimization_barrier(jnp.mean(wide * wide, axis=-1, keepdims=True)) + EPSILON)
    return (wide * factor * scales).astype(jnp.bfloat16)

def apply_rotation(values, token_positions):
    half_width = values.shape[-1] // 2
    frequency = ROPE_BASE ** (-2.0 * jnp.arange(half_width, dtype=jnp.float32) / values.shape[-1])
    angles = token_positions[..., None] * frequency
    cosine = jnp.concatenate([jnp.cos(angles), jnp.cos(angles)], axis=-1)
    sine_part = jnp.concatenate([jnp.sin(angles), jnp.sin(angles)], axis=-1)
    turned = jnp.concatenate([-values[..., half_width:], values[..., :half_width]], axis=-1)
    return values * cosine + turned * sine_part

def widened(array):
    return lax.optimization_barrier(array.astype(jnp.bfloat16)).astype(jnp.float32)

def reference(prompt_states, new_states, answer_cache, attn_gain, w_query, key_weight, value_weight, w_out, prompt_of, suffix_len):
    group_count = QUERY_HEADS // KEY_VALUE_HEADS
    score_scale = HEAD_WIDTH ** (-0.5)
    flat_prompts = prompt_states.reshape(2 * N_GRP, PROMPT_LENGTH, MODEL_WIDTH)
    group_width = QUERY_HEADS * HEAD_WIDTH // N_TP

    def prefill_one(token_rows):
        normed_states = normalize(token_rows, attn_gain)
        token_positions = jnp.arange(PROMPT_LENGTH, dtype=jnp.float32)[:, None]
        query_rows = apply_rotation(jnp.dot(normed_states, w_query, preferred_element_type=jnp.float32).reshape(PROMPT_LENGTH, QUERY_HEADS, HEAD_WIDTH), token_positions).astype(jnp.bfloat16)
        key_entries = apply_rotation(jnp.dot(normed_states, key_weight, preferred_element_type=jnp.float32).reshape(PROMPT_LENGTH, KEY_VALUE_HEADS, HEAD_WIDTH), token_positions).astype(jnp.bfloat16)
        value_entries = jnp.dot(normed_states, value_weight, preferred_element_type=jnp.float32).astype(jnp.bfloat16).reshape(PROMPT_LENGTH, KEY_VALUE_HEADS, HEAD_WIDTH)
        grouped_heads = query_rows.astype(jnp.float32).reshape(PROMPT_LENGTH, KEY_VALUE_HEADS, group_count, HEAD_WIDTH)
        scores = jnp.einsum('qkgd,skd->kgqs', grouped_heads, key_entries.astype(jnp.float32)) * score_scale
        causal = jnp.arange(PROMPT_LENGTH)[:, None] >= jnp.arange(PROMPT_LENGTH)[None, :]
        scores = jnp.where(causal, scores, -jnp.inf)
        row_peak = lax.optimization_barrier(jnp.max(scores, axis=-1, keepdims=True))
        expo = jnp.exp(scores - row_peak)
        totals = lax.optimization_barrier(jnp.sum(expo, axis=-1))
        mixed = jnp.einsum('kgqs,skd->qkgd', widened(expo), value_entries.astype(jnp.float32))
        mixed = mixed / jnp.transpose(totals, (2, 0, 1))[..., None]
        head_rows = mixed.astype(jnp.bfloat16).reshape(PROMPT_LENGTH, QUERY_HEADS * HEAD_WIDTH)
        result = token_rows.astype(jnp.float32)
        for member in range(N_TP):
            part_rows = head_rows[:, member * group_width:(member + 1) * group_width]
            part_weight = w_out[member * group_width:(member + 1) * group_width]
            result = result + widened(jnp.dot(part_rows, part_weight, preferred_element_type=jnp.float32))
        return (result.astype(jnp.bfloat16), key_entries, value_entries)
    prefill_rows, all_keys, all_values = lax.map(prefill_one, flat_prompts)
    prefill_out = prefill_rows.reshape(2, N_GRP, PROMPT_LENGTH, MODEL_WIDTH)
    total_count = 2 * SAMPLE_COUNT
    normed_fresh = normalize(new_states, attn_gain).reshape(total_count * 2, MODEL_WIDTH)
    token_positions = (PROMPT_LENGTH + suffix_len[:, :, None] + jnp.arange(2, dtype=jnp.int32)).astype(jnp.float32).reshape(total_count * 2, 1)
    fresh_query = apply_rotation(jnp.dot(normed_fresh, w_query, preferred_element_type=jnp.float32).reshape(total_count * 2, QUERY_HEADS, HEAD_WIDTH), token_positions).astype(jnp.bfloat16)
    fresh_query = fresh_query.reshape(total_count, 2, KEY_VALUE_HEADS, group_count, HEAD_WIDTH)
    fresh_keys = apply_rotation(jnp.dot(normed_fresh, key_weight, preferred_element_type=jnp.float32).reshape(total_count * 2, KEY_VALUE_HEADS, HEAD_WIDTH), token_positions).astype(jnp.bfloat16)
    fresh_keys = fresh_keys.reshape(total_count, 2, KEY_VALUE_HEADS, HEAD_WIDTH)
    fresh_values = jnp.dot(normed_fresh, value_weight, preferred_element_type=jnp.float32).astype(jnp.bfloat16).reshape(total_count, 2, KEY_VALUE_HEADS, HEAD_WIDTH)
    halves = (1 - jnp.arange(2, dtype=jnp.int32))[:, None] * N_GRP
    sources = (halves + prompt_of).reshape(total_count).astype(jnp.int32)
    cached_rows = answer_cache.reshape(total_count, SUFFIX_LENGTH, KEY_VALUE_HEADS, 2, HEAD_WIDTH)
    lengths = suffix_len.reshape(total_count).astype(jnp.int32)
    later = jnp.arange(2)[:, None] >= jnp.arange(2)[None, :]

    def decode_one(inputs):
        query_one, key_one, value_one, cache_one, source, length_one = inputs
        prefix_keys = lax.dynamic_index_in_dim(all_keys, source, 0, keepdims=False)
        prefix_values = lax.dynamic_index_in_dim(all_values, source, 0, keepdims=False)
        wide_query = query_one.astype(jnp.float32)
        score_pre = jnp.einsum('tkgd,lkd->tkgl', wide_query, prefix_keys.astype(jnp.float32)) * score_scale
        score_cache = jnp.einsum('tkgd,lkd->tkgl', wide_query, cache_one[:, :, 0].astype(jnp.float32)) * score_scale
        score_cache = jnp.where(jnp.arange(SUFFIX_LENGTH) < length_one, score_cache, -jnp.inf)
        score_new = jnp.einsum('tkgd,ukd->tkgu', wide_query, key_one.astype(jnp.float32)) * score_scale
        score_new = jnp.where(later[:, None, None, :], score_new, -jnp.inf)
        scores = jnp.concatenate([score_pre, score_cache, score_new], axis=-1)
        value_all = jnp.concatenate([prefix_values, cache_one[:, :, 1], value_one], axis=0).astype(jnp.float32)
        row_peak = lax.optimization_barrier(jnp.max(scores, axis=-1, keepdims=True))
        expo = jnp.exp(scores - row_peak)
        totals = lax.optimization_barrier(jnp.sum(expo, axis=-1))
        mixed = jnp.einsum('tkgl,lkd->tkgd', widened(expo), value_all) / totals[..., None]
        return mixed.astype(jnp.bfloat16).reshape(2, QUERY_HEADS * HEAD_WIDTH)
    decode_heads = lax.map(decode_one, (fresh_query, fresh_keys, fresh_values, cached_rows, sources, lengths))
    projected = jnp.dot(decode_heads.reshape(total_count * 2, QUERY_HEADS * HEAD_WIDTH), w_out, preferred_element_type=jnp.float32)
    decode_out = new_states.astype(jnp.float32) + projected.reshape(2, SAMPLE_COUNT, 2, MODEL_WIDTH)
    return (prefill_out, decode_out)
```

```python
import functools

import jax
import jax.numpy as jnp
from jax import lax
from jax.experimental import pallas as pl
from jax.experimental.pallas import tpu as pltpu
from jax.sharding import PartitionSpec as P

HEAD_WIDTH = 128
EPSILON = 1e-06
ROPE_BASE = 1000000.0
GROUP_STEPS = (4, 2, 1, 8)
VMEM_LIMIT = 40 * 1024 * 1024


def normalize(entries, scales):
    wide = entries.astype(jnp.float32)
    factor = lax.rsqrt(jnp.mean(wide * wide, axis=-1, keepdims=True) + EPSILON)
    return (wide * factor * scales).astype(jnp.bfloat16)


def rope_tables(positions):
    half = HEAD_WIDTH // 2
    frequency = ROPE_BASE ** (-2.0 * jnp.arange(half, dtype=jnp.float32) / HEAD_WIDTH)
    angles = positions.astype(jnp.float32)[:, None] * frequency
    cosine, sine = jnp.cos(angles), jnp.sin(angles)
    return jnp.concatenate([cosine, cosine], 1), jnp.concatenate([-sine, sine], 1)


def qkv_body(counts, steps, *refs):
    n = len(counts)
    xs, (wq, wk, wv, cos, sin, q_out, kv_out, acc) = refs[:n], refs[n:]
    step = pl.program_id(0)
    x = jnp.concatenate([r[...] for r in xs], axis=0) if n > 1 else xs[0][...]
    w = jnp.concatenate([wq[...], wk[...], wv[...]], axis=1)
    part = jnp.dot(x, w, preferred_element_type=jnp.float32)

    @pl.when(step == 0)
    def _():
        acc[...] = part

    @pl.when(step > 0)
    def _():
        acc[...] += part

    @pl.when(step == steps - 1)
    def _():
        c, s = cos[...], sin[...]
        wide = wq.shape[1]
        for h in range(wide // HEAD_WIDTH + 1):
            v = acc[:, h * HEAD_WIDTH : (h + 1) * HEAD_WIDTH]
            v = (v * c + pltpu.roll(v, HEAD_WIDTH // 2, 1) * s).astype(jnp.bfloat16)
            if h * HEAD_WIDTH < wide:
                q_out[:, h * HEAD_WIDTH : (h + 1) * HEAD_WIDTH] = v
            else:
                kv_out[:, :HEAD_WIDTH] = v
        kv_out[:, HEAD_WIDTH:] = acc[:, wide + HEAD_WIDTH :].astype(jnp.bfloat16)


def qkv(blocks, wq, wk, wv, tables):
    counts = [b.shape[0] for b in blocks]
    rows, depth = sum(counts), wq.shape[0]
    steps = 5 if depth % 640 == 0 else 1
    tile = depth // steps
    wide = wq.shape[1]
    whole = lambda shape: pl.BlockSpec(shape, lambda k: (0, 0))
    return pl.pallas_call(
        functools.partial(qkv_body, counts, steps),
        grid=(steps,),
        in_specs=[pl.BlockSpec((c, tile), lambda k: (0, k)) for c in counts]
        + [pl.BlockSpec((tile, w.shape[1]), lambda k: (k, 0)) for w in (wq, wk, wv)]
        + [whole((rows, HEAD_WIDTH))] * 2,
        out_specs=[whole((rows, wide)), whole((rows, 2 * HEAD_WIDTH))],
        out_shape=[
            jax.ShapeDtypeStruct((rows, wide), jnp.bfloat16),
            jax.ShapeDtypeStruct((rows, 2 * HEAD_WIDTH), jnp.bfloat16),
        ],
        scratch_shapes=[pltpu.VMEM((rows, wide + 2 * HEAD_WIDTH), jnp.float32)],
        compiler_params=pltpu.CompilerParams(vmem_limit_bytes=VMEM_LIMIT),
        cost_estimate=pl.CostEstimate(
            flops=2 * rows * depth * (wide + 256),
            bytes_accessed=2 * depth * (wide + 256 + rows),
            transcendentals=0,
        ),
    )(*blocks, wq, wk, wv, *tables)


def dot_t(a, b):
    return lax.dot_general(a, b, (((1,), (1,)), ((), ())), preferred_element_type=jnp.float32)


def simple_call(body, out_shape, flops, *args):
    nbytes = sum(a.size * a.dtype.itemsize for a in args)
    return pl.pallas_call(
        body,
        in_specs=[pl.BlockSpec(memory_space=pltpu.VMEM)] * len(args),
        out_specs=jax.tree.map(lambda _: pl.BlockSpec(memory_space=pltpu.VMEM), out_shape),
        out_shape=out_shape,
        compiler_params=pltpu.CompilerParams(vmem_limit_bytes=VMEM_LIMIT),
        cost_estimate=pl.CostEstimate(flops=flops, bytes_accessed=nbytes, transcendentals=0),
    )(*args)


def local_body(scale, q, kv, cache, lengths, out, stats):
    width, rows = HEAD_WIDTH, q.shape[0]
    groups, samples = q.shape[1] // width, cache.shape[0]
    slots = cache.shape[1]
    query = jnp.concatenate([q[:, g * width : (g + 1) * width] for g in range(groups)], axis=0)
    old = cache[...].reshape(samples * slots, 2 * width)
    total = groups * rows
    row = lax.broadcasted_iota(jnp.int32, (total, 1), 0) % rows
    column = lax.broadcasted_iota(jnp.int32, (1, samples * slots), 1)
    score_old = dot_t(query, old[:, :width]) * scale
    limit = row // 2 * slots + lengths[...]
    allowed = (column >= row // 2 * slots) & (column < limit)
    score_old = jnp.where(allowed, score_old, -jnp.inf)
    fresh = lax.broadcasted_iota(jnp.int32, (1, rows), 1)
    score_new = dot_t(query, kv[:, :width]) * scale
    score_new = jnp.where((fresh // 2 == row // 2) & (fresh <= row), score_new, -jnp.inf)
    peak = jnp.maximum(
        jnp.max(score_old, axis=1, keepdims=True), jnp.max(score_new, axis=1, keepdims=True)
    )
    expo_old, expo_new = jnp.exp(score_old - peak), jnp.exp(score_new - peak)
    both = jnp.sum(expo_old, axis=1, keepdims=True) + jnp.sum(expo_new, axis=1, keepdims=True)
    mixed = jnp.dot(
        expo_old.astype(jnp.bfloat16), old[:, width:], preferred_element_type=jnp.float32
    ) + jnp.dot(
        expo_new.astype(jnp.bfloat16), kv[:, width:], preferred_element_type=jnp.float32
    )
    out[...] = mixed
    lane = lax.broadcasted_iota(jnp.int32, stats.shape, 1)
    stats[...] = jnp.where(lane == 0, peak, both)


def local_attention(q, kv, cache, lengths, scale):
    total = q.shape[1] // HEAD_WIDTH * q.shape[0]
    shape = jax.ShapeDtypeStruct((total, HEAD_WIDTH), jnp.float32)
    flops = 4 * total * cache.shape[0] * cache.shape[1] * HEAD_WIDTH
    return simple_call(
        functools.partial(local_body, scale), (shape, shape), flops, q, kv, cache, lengths
    )


def prefix_body(scale, q, wanted, names, kv_a, kv_b, out):
    width, rows = HEAD_WIDTH, wanted.shape[0]
    groups = q.shape[1] // width
    chosen = (names[...] == wanted[...]).astype(jnp.bfloat16)
    picked = jnp.dot(chosen, q[...], preferred_element_type=jnp.float32).astype(jnp.bfloat16)
    query = jnp.concatenate([picked[:, g * width : (g + 1) * width] for g in range(groups)], axis=0)
    pairs = jnp.concatenate([kv_a[...], kv_b[...]], axis=0)
    score = dot_t(query, pairs[:, :width]) * scale
    peak = jnp.max(score, axis=1, keepdims=True)
    expo = jnp.exp(score - peak)
    both = jnp.sum(expo, axis=1, keepdims=True)
    mixed = jnp.dot(expo.astype(jnp.bfloat16), pairs[:, width:], preferred_element_type=jnp.float32)
    mixed = (mixed / both).astype(jnp.bfloat16)
    level = peak + jnp.log(both)
    lane = lax.broadcasted_iota(jnp.int32, (rows, width), 1)
    tail = jnp.zeros((rows, width), jnp.bfloat16)
    for g in range(groups):
        out[:, g * width : (g + 1) * width] = mixed[g * rows : (g + 1) * rows]
        rest = level[g * rows : (g + 1) * rows]
        for part in range(3):
            high = rest.astype(jnp.bfloat16)
            rest = rest - high.astype(jnp.float32)
            tail = jnp.where(lane == g * 3 + part, high, tail)
    out[:, groups * width :] = tail


def prefix_attention(q, wanted, names, kv_a, kv_b, scale):
    rows = wanted.shape[0]
    shape = jax.ShapeDtypeStruct((rows, q.shape[1] + HEAD_WIDTH), jnp.bfloat16)
    return simple_call(
        functools.partial(prefix_body, scale), shape, 100_000_000, q, wanted, names, kv_a, kv_b
    )


def merge_body(back, wanted, names, local, stats, out):
    width, rows = HEAD_WIDTH, wanted.shape[0]
    groups = local.shape[0] // rows
    chosen = (names[...] == wanted[...]).astype(jnp.bfloat16)
    picked = jnp.dot(chosen, back[...], preferred_element_type=jnp.float32)
    tail = picked[:, groups * width :]
    for g in range(groups):
        level = tail[:, g * 3 : g * 3 + 1] + tail[:, g * 3 + 1 : g * 3 + 2]
        level = level + tail[:, g * 3 + 2 : g * 3 + 3]
        peak = stats[g * rows : (g + 1) * rows, 0:1]
        both = stats[g * rows : (g + 1) * rows, 1:2]
        top = jnp.maximum(level, peak)
        factor_pre, factor_loc = jnp.exp(level - top), jnp.exp(peak - top)
        total = factor_pre + both * factor_loc
        mixed = picked[:, g * width : (g + 1) * width] * factor_pre
        mixed = mixed + local[g * rows : (g + 1) * rows] * factor_loc
        out[:, g * width : (g + 1) * width] = (mixed / total).astype(jnp.bfloat16)


def merge(back, wanted, names, local, stats):
    rows = wanted.shape[0]
    shape = jax.ShapeDtypeStruct((rows, back.shape[1] - HEAD_WIDTH), jnp.bfloat16)
    return simple_call(merge_body, shape, 10_000_000, back, wanted, names, local, stats)


def prefill_body(scale, mine_a, mine_b, q_a, q_b, kv_a, kv_b, place_row, place_column, own, other):
    width = HEAD_WIDTH
    groups = q_a.shape[1] // width
    pairs = jnp.concatenate([kv_a[...], kv_b[...]], axis=0)
    allowed = place_row[...] >= place_column[...]
    count_a, count_b = q_a.shape[0], q_b.shape[0]
    for g in range(groups):
        cols = slice(g * width, (g + 1) * width)
        query = jnp.concatenate([q_a[:, cols], q_b[:, cols]], axis=0)
        score = jnp.where(allowed, dot_t(query, pairs[:, :width]) * scale, -jnp.inf)
        expo = jnp.exp(score - jnp.max(score, axis=1, keepdims=True))
        both = jnp.sum(expo, axis=1, keepdims=True)
        mixed = jnp.dot(
            expo.astype(jnp.bfloat16), pairs[:, width:], preferred_element_type=jnp.float32
        )
        mixed = (mixed / both).astype(jnp.bfloat16)
        own[:mine_a, cols] = mixed[:mine_a]
        other[:mine_a, cols] = mixed[mine_a:count_a]
        own[mine_a:, cols] = mixed[count_a : count_a + mine_b]
        other[mine_a:, cols] = mixed[count_a + mine_b :]


def prefill_attention(q_a, q_b, kv_a, kv_b, places, scale):
    mine_a, mine_b = q_a.shape[0] // 2, q_b.shape[0] // 2
    shape = jax.ShapeDtypeStruct((mine_a + mine_b, q_a.shape[1]), jnp.bfloat16)
    length = q_a.shape[0] + q_b.shape[0]
    return simple_call(
        functools.partial(prefill_body, scale, mine_a, mine_b),
        (shape, shape),
        4 * length * length * q_a.shape[1],
        q_a, q_b, kv_a, kv_b, places[:, None], places[None, :],
    )


def out_body(own, other, w_own, w_other, *outs):
    part = jnp.dot(own[...], w_own[...], preferred_element_type=jnp.float32)
    part = part + jnp.dot(other[...], w_other[...], preferred_element_type=jnp.float32)
    rows = outs[0].shape[0]
    for i, out in enumerate(outs):
        out[...] = part[i * rows : (i + 1) * rows].astype(out.dtype)


def out_projection(own, other, w_own, w_other, block, dtype):
    rows, depth = own.shape
    wide = w_own.shape[1]
    tile = 512 if wide % 512 == 0 else wide
    count = rows // block
    return pl.pallas_call(
        out_body,
        grid=(wide // tile,),
        in_specs=[pl.BlockSpec((rows, depth), lambda n: (0, 0))] * 2
        + [pl.BlockSpec((depth, tile), lambda n: (0, n))] * 2,
        out_specs=[pl.BlockSpec((block, tile), lambda n: (0, n))] * count,
        out_shape=[jax.ShapeDtypeStruct((block, wide), dtype)] * count,
        compiler_params=pltpu.CompilerParams(vmem_limit_bytes=VMEM_LIMIT),
        cost_estimate=pl.CostEstimate(
            flops=4 * rows * depth * wide,
            bytes_accessed=4 * depth * wide + 2 * rows * wide,
            transcendentals=0,
        ),
    )(own, other, w_own, w_other)


def partial_body(heads, w, out):
    out[...] = jnp.dot(heads[...], w[...], preferred_element_type=jnp.float32).astype(out.dtype)


def partial_projection(heads, w):
    rows, depth = heads.shape
    wide = w.shape[1]
    tile = 1024 if wide % 1024 == 0 else wide
    return pl.pallas_call(
        partial_body,
        grid=(wide // tile,),
        in_specs=[
            pl.BlockSpec((rows, depth), lambda n: (0, 0)),
            pl.BlockSpec((depth, tile), lambda n: (0, n)),
        ],
        out_specs=pl.BlockSpec((rows, tile), lambda n: (0, n)),
        out_shape=jax.ShapeDtypeStruct((rows, wide), jnp.bfloat16),
        compiler_params=pltpu.CompilerParams(vmem_limit_bytes=VMEM_LIMIT),
        cost_estimate=pl.CostEstimate(
            flops=2 * rows * depth * wide, bytes_accessed=2 * depth * wide, transcendentals=0
        ),
    )(heads, w)


def shards(
    prompt_states,
    new_states,
    answer_cache,
    attn_gain,
    w_query,
    key_weight,
    value_weight,
    w_out,
    prompt_of,
    suffix_len,
):
    scale = HEAD_WIDTH ** (-0.5)
    rows = prompt_states[0, 0]
    block, width = rows.shape
    tp, grp = lax.axis_index("tp"), lax.axis_index("grp")
    y, core = tp // 2, tp % 2
    tp_size, grp_size = lax.axis_size("tp"), lax.axis_size("grp")
    chips = tp_size // 2

    def around(value, by):
        return lax.ppermute(value, "tp", [(i, (i + 2 * by) % tp_size) for i in range(tp_size)])

    def swap(value, axis, mask):
        return lax.ppermute(value, axis, [(i, i ^ mask) for i in range(lax.axis_size(axis))])

    normed = normalize(rows, attn_gain)
    from_down = around(normed, 1)
    from_up = around(normed, -1)
    mate_own = swap(normed, "tp", 1)

    samples = new_states.shape[1]
    lengths = suffix_len[0]
    tokens = new_states[0].reshape(samples * 2, width)
    fresh_places = (
        block * tp_size + lengths[:, None] + jnp.arange(2, dtype=jnp.int32)
    ).reshape(samples * 2)
    fresh_q, fresh_kv = qkv(
        [normalize(tokens, attn_gain)], w_query, key_weight, value_weight, rope_tables(fresh_places)
    )
    gathered = fresh_q
    order = [0]
    for mask in GROUP_STEPS:
        gathered = jnp.concatenate([gathered, swap(gathered, "grp", mask)], axis=0)
        order = order + [k ^ mask for k in order]
    owners = jnp.bitwise_xor(jnp.array(order, dtype=jnp.int32), grp)
    names = (owners[:, None] * (samples * 2) + jnp.arange(samples * 2, dtype=jnp.int32)).reshape(
        1, -1
    )
    w_mate = swap(w_out, "tp", 1)

    half = block // 2
    ahead = around(from_down[:half], 1)
    behind = around(from_up[half:], -1)
    mate_down = swap(from_down, "tp", 1)
    mate_up = swap(from_up, "tp", 1)
    far = jnp.concatenate([ahead, behind], axis=0)
    mate_far = swap(far, "tp", 1)

    prompts = prompt_of[0]
    index = jnp.arange(prompts.shape[0], dtype=jnp.int32)
    same = prompts[:, None] == prompts[None, :]
    rank = jnp.sum((same & (index[None, :] < index[:, None])).astype(jnp.int32), axis=1)
    slot = jnp.arange(samples, dtype=jnp.int32)
    hit = (prompts == grp)[None, :] & (rank[None, :] == slot[:, None])
    sought = jnp.sum(jnp.where(hit, index[None, :], 0), axis=1)
    pair = jnp.arange(2, dtype=jnp.int32)
    wanted = (sought[:, None] * 2 + pair).reshape(samples * 2, 1)
    home = lax.dynamic_slice_in_dim(prompts * samples + rank, grp * samples, samples)
    returned = (home[:, None] * 2 + pair).reshape(samples * 2, 1)
    groups = w_query.shape[1] // HEAD_WIDTH
    limits = jnp.tile(jnp.repeat(lengths, 2), groups)[:, None]

    turns = jnp.array([0, -1, 1, 2], dtype=jnp.int32)
    chip = (y + turns) % chips
    inside = jnp.arange(block, dtype=jnp.int32)
    mine = ((2 * chip + core) * block)[:, None] + inside
    theirs = ((2 * chip + 1 - core) * block)[:, None] + inside
    places_a = jnp.concatenate([mine[:3].reshape(-1), theirs[:3].reshape(-1)])
    places_b = jnp.concatenate([mine[3], theirs[3]])
    places = jnp.concatenate([places_a, places_b])

    weights = (w_query, key_weight, value_weight)
    q_a, kv_a = qkv(
        [normed, from_down, from_up, mate_own, mate_down, mate_up], *weights, rope_tables(places_a)
    )
    handed_a = swap(kv_a, "role", 1)
    q_b, kv_b = qkv([far, mate_far], *weights, rope_tables(places_b))
    handed_b = swap(kv_b, "role", 1)

    local, stats = local_attention(fresh_q, fresh_kv, answer_cache[0], limits, scale)

    heads_own, heads_other = prefill_attention(q_a, q_b, kv_a, kv_b, places, scale)
    heads_mate = swap(heads_other, "tp", 1)
    near = 3 * block
    to_own, to_down, to_up, to_far = out_projection(
        heads_own, heads_mate, w_out, w_mate, block, jnp.bfloat16
    )
    sum_far = around(to_far, 2)
    sum_up = around(to_up, 1)
    sum_down = around(to_down, -1)

    answered = prefix_attention(gathered, wanted, names, handed_a, handed_b, scale)
    spread = jnp.broadcast_to(answered[None], (grp_size,) + answered.shape)
    back = lax.all_to_all(spread, "grp", 0, 0, tiled=False)
    back = back.reshape(grp_size * samples * 2, -1)
    decoded = merge(
        back, returned, jnp.arange(back.shape[0], dtype=jnp.int32)[None, :], local, stats
    )
    partial = partial_projection(decoded, w_out)
    kept = lax.dynamic_slice_in_dim(partial, core * samples, samples)
    given = lax.dynamic_slice_in_dim(partial, (1 - core) * samples, samples)
    taken = swap(given, "tp", 1)
    level = lax.optimization_barrier(
        (kept.astype(jnp.float32) + taken.astype(jnp.float32)).astype(jnp.bfloat16)
    )
    taken = swap(level, "tp", 2)
    level = lax.optimization_barrier(
        (level.astype(jnp.float32) + taken.astype(jnp.float32)).astype(jnp.bfloat16)
    )
    taken = swap(level, "tp", 4)
    summed = level.astype(jnp.float32) + taken.astype(jnp.float32)
    theirs_sum = swap(summed, "tp", 1)
    low = jnp.where(core == 0, summed, theirs_sum)
    high = jnp.where(core == 0, theirs_sum, summed)
    total = jnp.concatenate([low, high], axis=0)
    decode_out = tokens.astype(jnp.float32) + total

    prefill_out = (
        rows.astype(jnp.float32)
        + to_own.astype(jnp.float32)
        + sum_far.astype(jnp.float32)
        + sum_up.astype(jnp.float32)
        + sum_down.astype(jnp.float32)
    ).astype(jnp.bfloat16)
    return prefill_out[None, None], decode_out.reshape(1, samples, 2, width)


def solution(mesh):
    placed = (
        P("role", "grp", "tp", None),
        P("role", "grp", None, None),
        P("role", "grp", None, "tp"),
        P(),
        P(None, "tp"),
        P(None, "tp"),
        P(None, "tp"),
        P("tp", None),
        P("role", None),
        P("role", "grp"),
    )
    return jax.shard_map(
        shards,
        mesh=mesh,
        in_specs=placed,
        out_specs=(P("role", "grp", "tp", None), P("role", "grp", None, None)),
        check_vma=False,
    )
```

```python
import functools

import jax
import jax.numpy as jnp
import numpy as np
from jax import lax
from jax.experimental import pallas as pl
from jax.experimental.pallas import tpu as pltpu
from jax.sharding import PartitionSpec as P

HEAD_WIDTH = 128
EPSILON = 1e-06
ROPE_BASE = 1000000.0
VMEM_LIMIT = 14 * 1024 * 1024
FIRST, SECOND, THIRD, FOURTH = 4, 1, 2, 8
HELD = (0, FIRST, SECOND, FIRST ^ SECOND)
SERVED = (0, THIRD, FOURTH, THIRD ^ FOURTH)


def fixed_tables(start, length):
    spans = np.concatenate([np.arange(HEAD_WIDTH // 2)] * 2)
    angles = np.arange(start, start + length)[:, None] * ROPE_BASE ** (-2.0 * spans / HEAD_WIDTH)
    sign = np.where(np.arange(HEAD_WIDTH) < HEAD_WIDTH // 2, -1.0, 1.0)
    return np.concatenate([np.cos(angles), np.sin(angles) * sign], axis=1).astype(np.float32)


VMEM = pl.BlockSpec(memory_space=pltpu.VMEM)
SMEM = pl.BlockSpec(memory_space=pltpu.SMEM)
ANY = pl.BlockSpec(memory_space=pl.ANY)
HBM = pl.BlockSpec(memory_space=pltpu.HBM)


def simple_call(body, out_shape, flops, *args, specs=None, scratch=()):
    nbytes = sum(a.size * a.dtype.itemsize for a in args)
    return pl.pallas_call(
        body,
        in_specs=specs or [VMEM] * len(args),
        out_specs=jax.tree.map(lambda _: VMEM, out_shape),
        out_shape=out_shape,
        scratch_shapes=list(scratch),
        compiler_params=pltpu.CompilerParams(vmem_limit_bytes=VMEM_LIMIT),
        cost_estimate=pl.CostEstimate(flops=flops, bytes_accessed=nbytes if flops else 0, transcendentals=0),
    )(*args)


def normalized(wide, gain):
    factor = lax.rsqrt(jnp.mean(wide * wide, axis=-1, keepdims=True) + EPSILON)
    return (wide * factor * gain).astype(jnp.bfloat16)


def fetch(sources, targets, sems):
    copies = [
        pltpu.make_async_copy(source, target, sems.at[i])
        for i, (source, target) in enumerate(zip(sources, targets))
    ]
    for copy in copies:
        copy.start()
    return copies


def like(*arrays):
    held = [pltpu.VMEM(a.shape, a.dtype) for a in arrays]
    return held + [pltpu.SemaphoreType.DMA((len(arrays),))]


def norm_body(tp, grp, x_far, gain_far, out, x, gain, sems):
    for copy in fetch((x_far, gain_far), (x, gain), sems):
        copy.wait()
    for i in range(x.shape[0] // 16):
        part = slice(i * 16, (i + 1) * 16)
        out[part] = normalized(x[part].astype(jnp.float32), gain[...])


def row_lengths(lengths, rows):
    samples = lengths.shape[1]
    row = lax.broadcasted_iota(jnp.int32, (rows, samples), 0)
    own = lax.broadcasted_iota(jnp.int32, (rows, samples), 1) == row // 2
    wide = jnp.where(own, lengths[...].astype(jnp.float32), 0.0)
    return jnp.sum(wide, axis=1, keepdims=True).astype(jnp.int32)


def fresh_body(samples, where, *refs):
    count = 5
    far, (out, c_out, s_out, forth, back) = refs[:count], refs[count : 2 * count]
    near, (wide, spots, sems) = refs[2 * count : 3 * count], refs[3 * count :]
    copies = fetch(far, near, sems)
    x, gain, lengths, table, prompts = near
    copies[4].wait()
    route(samples, where[0], prompts, forth, back, spots)
    for copy in copies[:4]:
        copy.wait()
    rows = out.shape[0]
    for i in range(x.shape[0]):
        wide[2 * i : 2 * i + 2] = x[i].astype(jnp.float32)
    for i in range(rows // 16):
        part = slice(i * 16, (i + 1) * 16)
        out[part] = normalized(wide[part], gain[...])
    shape = (rows, table.shape[0])
    row = lax.broadcasted_iota(jnp.int32, shape, 0)
    column = lax.broadcasted_iota(jnp.int32, shape, 1)
    at = (column == row_lengths(lengths, rows) + row % 2).astype(jnp.float32)
    both = jnp.dot(at, table[...], precision=lax.Precision.HIGHEST)
    c_out[...] = both[:, :HEAD_WIDTH]
    s_out[...] = both[:, HEAD_WIDTH:]


def prepare_fresh(grp, x, gain, lengths, table, prompts):
    samples, width = x.shape[0], x.shape[2]
    rows, wide = 2 * samples, 8 * samples
    flat = jax.ShapeDtypeStruct((rows, HEAD_WIDTH), jnp.float32)
    choice = jax.ShapeDtypeStruct((wide, wide), jnp.bfloat16)
    far = (x, gain.reshape(1, -1), lengths, jnp.asarray(table), prompts)
    *held, sems = like(*far)
    return simple_call(
        functools.partial(fresh_body, samples),
        (jax.ShapeDtypeStruct((rows, width), jnp.bfloat16), flat, flat, choice, choice),
        1_000_000, grp, *far,
        specs=[SMEM] + [HBM] * 5,
        scratch=held
        + [
            pltpu.VMEM((rows, width), jnp.float32),
            pltpu.VMEM((2 * prompts.shape[1], wide), jnp.float32),
            sems,
        ],
    )


def norm_prompt(x, gain, tp, grp):
    shape = jax.ShapeDtypeStruct(x.shape, jnp.bfloat16)
    far = (x, gain.reshape(1, -1))
    return simple_call(
        norm_body, shape, 1_000_000, tp, grp, *far,
        specs=[SMEM] * 2 + [HBM] * 2, scratch=like(*far),
    )


def route(samples, grp, prompts, forth, back, spots):
    rows, count = 2 * samples, prompts.shape[1]
    wide = 2 * count
    wide_prompts = prompts[...].astype(jnp.float32)

    def grid(shape, axis):
        return lax.broadcasted_iota(jnp.int32, shape, axis)

    spread = (grid((count, wide), 1) // 2 == grid((count, wide), 0)).astype(jnp.bfloat16)
    across = jnp.dot(
        jnp.broadcast_to(wide_prompts, (8, count)).astype(jnp.bfloat16),
        spread,
        preferred_element_type=jnp.float32,
    )[:1]
    own = grid((wide, count), 1) == grid((wide, count), 0) // 2
    down = jnp.sum(jnp.where(own, wide_prompts, 0.0), axis=1, keepdims=True)
    earlier = (across == down) & (grid((wide, wide), 1) < grid((wide, wide), 0))
    rank = jnp.sum(earlier.astype(jnp.float32), axis=1, keepdims=True)
    spots[...] = jnp.broadcast_to(down * rows + rank, spots.shape)

    def cells(masks):
        parts = [spots[pl.ds(pl.multiple_of((grp ^ m) * rows, rows), rows)] for m in masks]
        return jnp.concatenate(parts, axis=0)

    def names(masks):
        column = grid((1, 4 * rows), 1)
        start = jnp.zeros((1, 4 * rows), jnp.int32)
        for i, m in enumerate(masks):
            start = jnp.where(column // rows == i, (grp ^ m) * rows, start)
        return (start + column % rows).astype(jnp.float32)

    picked = (cells(HELD) == names(SERVED)).astype(jnp.float32)
    forth[...] = picked.T.astype(jnp.bfloat16)
    back[...] = (cells(SERVED) == names(HELD)).astype(jnp.bfloat16)


def hold(values, after):
    count = len(values)
    return pl.pallas_call(
        lambda *refs: None,
        in_specs=[ANY] * (count + len(after)),
        out_specs=[ANY] * count,
        out_shape=[jax.ShapeDtypeStruct(v.shape, v.dtype) for v in values],
        input_output_aliases={i: i for i in range(count)},
        compiler_params=pltpu.CompilerParams(vmem_limit_bytes=VMEM_LIMIT),
        cost_estimate=pl.CostEstimate(flops=0, bytes_accessed=0, transcendentals=0),
    )(*values, *after)


def join_body(a, b, *rest):
    out = rest[-1]
    out[: a.shape[0]] = a[...]
    out[a.shape[0] :] = b[...]


def pick_body(choice, near, far, *rest):
    kept, third, fourth = rest[-3:]
    rows = kept.shape[0]
    held = jnp.concatenate([near[...], far[...]], axis=0)
    picked = jnp.dot(choice[...], held, preferred_element_type=jnp.float32).astype(jnp.bfloat16)
    kept[...] = picked[:rows]
    third[:rows] = picked[rows : 2 * rows]
    third[rows:] = picked[3 * rows :]
    fourth[...] = picked[2 * rows : 3 * rows]


def pass_body(part, came, *rest):
    out = rest[-1]
    rows = part.shape[0]
    out[...] = part[...] + came[rows:]


def exchange_near(value, swap, after):
    shape = jax.ShapeDtypeStruct((2 * value.shape[0], value.shape[1]), value.dtype)
    args = (value, swap(value, "grp", FIRST))
    specs = [VMEM] * 2 + [ANY] * len(after)
    return simple_call(join_body, shape, 0, *args, *after, specs=specs)


def exchange_pick(near, choice, swap, after):
    rows, wide = near.shape[0] // 2, near.shape[1]
    shape = lambda n: jax.ShapeDtypeStruct((n * rows, wide), near.dtype)
    args = (choice, near, swap(near, "grp", SECOND))
    return simple_call(
        pick_body, (shape(1), shape(2), shape(1)), 0, *args, *after,
        specs=[VMEM] * 3 + [ANY] * len(after),
    )


def exchange_pass(third, fourth, swap, after):
    came = swap(third, "grp", THIRD)
    shape = jax.ShapeDtypeStruct(fourth.shape, fourth.dtype)
    specs = [VMEM] * 2 + [ANY] * len(after)
    return came, simple_call(pass_body, shape, 0, fourth, came, *after, specs=specs)


def arrived(kept, came, last):
    return kept[...] + came[: kept.shape[0]] + last[...]


def cut_body(a, b, top, low):
    half = top.shape[0]
    top[...] = a[:half]
    low[...] = b[half:]


def cut(a, b):
    shape = jax.ShapeDtypeStruct((a.shape[0] // 2, a.shape[1]), a.dtype)
    return simple_call(cut_body, (shape, shape), 0, a, b)


TURNS = (0, 0, -1, 1, -1, 1, 2, 2)
FLIPS = (0, 1, 0, 0, 1, 1, 0, 1)


def start_of(tp, chips, block, i):
    chip = lax.rem(tp // 2 + TURNS[i] + chips, chips)
    return (2 * chip + ((tp % 2) ^ FLIPS[i])) * block


def rotate(acc, c, s, q_out, kv_out, base):
    wide = q_out.shape[1]
    for h in range(wide // HEAD_WIDTH + 1):
        v = acc[:, h * HEAD_WIDTH : (h + 1) * HEAD_WIDTH]
        v = (v * c + pltpu.roll(v, HEAD_WIDTH // 2, 1) * s).astype(jnp.bfloat16)
        if h * HEAD_WIDTH == wide:
            kv_out[base:, :HEAD_WIDTH] = v
        else:
            q_out[base:, h * HEAD_WIDTH : (h + 1) * HEAD_WIDTH] = v
    kv_out[base:, HEAD_WIDTH:] = acc[:, wide + HEAD_WIDTH :].astype(jnp.bfloat16)


def chunks(depth):
    count = 5 if depth % 640 == 0 else 1
    return [slice(i * depth // count, (i + 1) * depth // count) for i in range(count)]


def fresh_qkv_body(x, wq, wk, wv, cos, sin, q_out, kv_out, joined, acc, sems):
    copies = []
    for i, part in enumerate(chunks(x.shape[1])):
        at = 0
        for j, w in enumerate((wq, wk, wv)):
            target = joined.at[part, at : at + w.shape[1]]
            at += w.shape[1]
            copies.append(pltpu.make_async_copy(w.at[part], target, sems.at[i, j]))
            copies[-1].start()
    for i, part in enumerate(chunks(x.shape[1])):
        for j in range(3):
            copies[3 * i + j].wait()
        piece = jnp.dot(x[:, part], joined[part], preferred_element_type=jnp.float32)
        acc[...] = piece if i == 0 else acc[...] + piece
    rotate(acc, cos[...], sin[...], q_out, kv_out, 0)


def fresh_qkv(x, weights, tables):
    rows, depth = x.shape
    total = sum(w.shape[1] for w in weights)
    shape = lambda *dims: jax.ShapeDtypeStruct(dims, jnp.bfloat16)
    return simple_call(
        fresh_qkv_body,
        (shape(rows, total - 2 * HEAD_WIDTH), shape(rows, 2 * HEAD_WIDTH), shape(depth, total)),
        2 * rows * depth * total, x, *weights, *tables,
        specs=[VMEM] + [HBM] * 3 + [VMEM] * 2,
        scratch=[
            pltpu.VMEM((rows, total), jnp.float32),
            pltpu.SemaphoreType.DMA((len(chunks(depth)), 3)),
        ],
    )


def qkv_body(n, first, block, early, skip, *refs):
    xs, (w, table, where, *rest) = refs[:n], refs[n:]
    q_out, kv_out, acc = rest[-3:]
    for i, part in enumerate(chunks(w.shape[0])):
        x = jnp.concatenate([r[:, part] for r in xs], axis=0)
        piece = jnp.dot(x, w[part], preferred_element_type=jnp.float32)
        acc[...] = piece if i == 0 else acc[...] + piece
    base = 0
    if early:
        q_early, kv_early = rest[:2]
        base = q_early.shape[0]
        q_out[:base] = q_early[...]
        kv_out[:base] = kv_early[...]
    chips = table.shape[0] // block // 2
    spots = [start_of(where[0], chips, block, first + i) for i in range(acc.shape[0] // block)]
    spots = [pl.ds(pl.multiple_of(spot, block), block) for spot in spots]
    both = jnp.concatenate([table[spot] for spot in spots], axis=0)
    rotate(acc, both[:, :HEAD_WIDTH], both[:, HEAD_WIDTH:], q_out, kv_out, base)


def qkv(blocks, joined, table, where, first, block, early=(), after=()):
    rows, (depth, total) = sum(b.shape[0] for b in blocks), joined.shape
    base = early[0].shape[0] if early else 0
    shape = lambda wide: jax.ShapeDtypeStruct((base + rows, wide), jnp.bfloat16)
    return simple_call(
        functools.partial(qkv_body, len(blocks), first, block, bool(early), len(after)),
        (shape(total - 2 * HEAD_WIDTH), shape(2 * HEAD_WIDTH)),
        2 * rows * depth * total, *blocks, joined, jnp.asarray(table), where, *early, *after,
        specs=[VMEM] * (len(blocks) + 2) + [SMEM] + [VMEM] * len(early) + [ANY] * len(after),
        scratch=[pltpu.VMEM((rows, total), jnp.float32)],
    )


def dot_t(a, b):
    return lax.dot_general(a, b, (((1,), (1,)), ((), ())), preferred_element_type=jnp.float32)


def local_body(scale, q, kv, cache_far, lengths_far, after, out, stats, cache, lengths, sems):
    copies = fetch((cache_far, lengths_far), (cache, lengths), sems)
    for copy in copies:
        copy.wait()
    width, rows = HEAD_WIDTH, q.shape[0]
    groups, samples = q.shape[1] // width, cache.shape[0]
    slots = cache.shape[1]
    query = jnp.concatenate(
        [q[:, g * width : (g + 1) * width] for g in range(groups)], axis=0
    )
    old = cache[...].reshape(samples * slots, 2 * width)
    total = groups * rows
    row = lax.broadcasted_iota(jnp.int32, (total, 1), 0) % rows
    column = lax.broadcasted_iota(jnp.int32, (1, samples * slots), 1)
    score_old = dot_t(query, old[:, :width]) * scale
    limit = row // 2 * slots + jnp.concatenate([row_lengths(lengths, rows)] * groups, axis=0)
    allowed = (column >= row // 2 * slots) & (column < limit)
    score_old = jnp.where(allowed, score_old, -jnp.inf)
    fresh = lax.broadcasted_iota(jnp.int32, (1, rows), 1)
    score_new = dot_t(query, kv[:, :width]) * scale
    score_new = jnp.where((fresh // 2 == row // 2) & (fresh <= row), score_new, -jnp.inf)
    peak = jnp.maximum(
        jnp.max(score_old, axis=1, keepdims=True), jnp.max(score_new, axis=1, keepdims=True)
    )
    expo_old, expo_new = jnp.exp(score_old - peak), jnp.exp(score_new - peak)
    both = jnp.sum(expo_old, axis=1, keepdims=True) + jnp.sum(expo_new, axis=1, keepdims=True)
    mixed = jnp.dot(
        expo_old.astype(jnp.bfloat16), old[:, width:], preferred_element_type=jnp.float32
    ) + jnp.dot(
        expo_new.astype(jnp.bfloat16), kv[:, width:], preferred_element_type=jnp.float32
    )
    out[...] = mixed
    lane = lax.broadcasted_iota(jnp.int32, stats.shape, 1)
    stats[...] = jnp.where(lane == 0, peak, both)


def local_attention(q, kv, cache, lengths, scale, after):
    total = q.shape[1] // HEAD_WIDTH * q.shape[0]
    shape = jax.ShapeDtypeStruct((total, HEAD_WIDTH), jnp.float32)
    flops = 4 * total * cache.shape[0] * cache.shape[1] * HEAD_WIDTH
    return simple_call(
        functools.partial(local_body, scale), (shape, shape), flops,
        q, kv, cache, lengths, after,
        specs=[VMEM] * 2 + [HBM] * 2 + [ANY], scratch=like(cache, lengths),
    )


def prefix_body(scale, kept, came, last, kv_a, kv_b, after, out):
    width, rows = HEAD_WIDTH, kept.shape[0]
    groups = kept.shape[1] // width
    picked = arrived(kept, came, last)
    query = jnp.concatenate([picked[:, g * width : (g + 1) * width] for g in range(groups)], axis=0)
    pairs = jnp.concatenate([kv_a[...], kv_b[...]], axis=0)
    score = dot_t(query, pairs[:, :width]) * scale
    peak = jnp.max(score, axis=1, keepdims=True)
    expo = jnp.exp(score - peak)
    both = jnp.sum(expo, axis=1, keepdims=True)
    mixed = jnp.dot(expo.astype(jnp.bfloat16), pairs[:, width:], preferred_element_type=jnp.float32)
    mixed = (mixed / both).astype(jnp.bfloat16)
    level = peak + jnp.log(both)
    lane = lax.broadcasted_iota(jnp.int32, (rows, width), 1)
    tail = jnp.zeros((rows, width), jnp.bfloat16)
    for g in range(groups):
        out[:, g * width : (g + 1) * width] = mixed[g * rows : (g + 1) * rows]
        rest = level[g * rows : (g + 1) * rows]
        for part in range(3):
            high = rest.astype(jnp.bfloat16)
            rest = rest - high.astype(jnp.float32)
            tail = jnp.where(lane == g * 3 + part, high, tail)
    out[:, groups * width :] = tail


def prefix_attention(asked, kv_a, kv_b, scale, after):
    rows, wide = asked[0].shape
    shape = jax.ShapeDtypeStruct((rows, wide + HEAD_WIDTH), jnp.bfloat16)
    return simple_call(
        functools.partial(prefix_body, scale), shape, 100_000_000, *asked, kv_a, kv_b, after,
        specs=[VMEM] * 5 + [ANY],
    )


def merge_body(kept, came, last, local, stats, *rest):
    out = rest[-1]
    width, rows = HEAD_WIDTH, kept.shape[0]
    groups = local.shape[0] // rows
    picked = arrived(kept, came, last).astype(jnp.float32)
    tail = picked[:, groups * width :]
    for g in range(groups):
        level = tail[:, g * 3 : g * 3 + 1] + tail[:, g * 3 + 1 : g * 3 + 2]
        level = level + tail[:, g * 3 + 2 : g * 3 + 3]
        peak = stats[g * rows : (g + 1) * rows, 0:1]
        both = stats[g * rows : (g + 1) * rows, 1:2]
        top = jnp.maximum(level, peak)
        factor_pre, factor_loc = jnp.exp(level - top), jnp.exp(peak - top)
        total = factor_pre + both * factor_loc
        mixed = picked[:, g * width : (g + 1) * width] * factor_pre
        mixed = mixed + local[g * rows : (g + 1) * rows] * factor_loc
        out[:, g * width : (g + 1) * width] = (mixed / total).astype(jnp.bfloat16)


def merge(back, local, stats, after):
    rows, wide = back[0].shape
    shape = jax.ShapeDtypeStruct((rows, wide - HEAD_WIDTH), jnp.bfloat16)
    return simple_call(
        merge_body, shape, 0, *back, local, stats, *after,
        specs=[VMEM] * 5 + [ANY] * len(after),
    )


def prefill_body(scale, q_a, q_b, kv_a, kv_b, where, *rest):
    own, other = rest[-2:]
    width = HEAD_WIDTH
    groups = q_a.shape[1] // width
    block = own.shape[0] // 4
    pairs = jnp.concatenate([kv_a[...], kv_b[...]], axis=0)
    length = pairs.shape[0]

    def places(shape, axis):
        spot = lax.broadcasted_iota(jnp.int32, shape, axis)
        shift = jnp.zeros(shape, jnp.int32)
        count = length // block
        for i in range(count):
            start = start_of(where[0], count // 2, block, i)
            shift = jnp.where(spot // block == i, start - i * block, shift)
        return spot + shift

    allowed = places((length, 1), 0) >= places((1, length), 1)
    for g in range(groups):
        cols = slice(g * width, (g + 1) * width)
        query = jnp.concatenate([q_a[:, cols], q_b[:, cols]], axis=0)
        score = jnp.where(allowed, dot_t(query, pairs[:, :width]) * scale, -jnp.inf)
        expo = jnp.exp(score - jnp.max(score, axis=1, keepdims=True))
        both = jnp.sum(expo, axis=1, keepdims=True)
        mixed = jnp.dot(
            expo.astype(jnp.bfloat16), pairs[:, width:], preferred_element_type=jnp.float32
        )
        mixed = (mixed / both).astype(jnp.bfloat16)
        part = lambda i, n: mixed[i * block : (i + n) * block]
        for out, at in ((own, (0, 2, 6)), (other, (1, 4, 7))):
            out[:block, cols] = part(at[0], 1)
            out[block : 3 * block, cols] = part(at[1], 2)
            out[3 * block :, cols] = part(at[2], 1)


def prefill_attention(q_a, q_b, kv_a, kv_b, where, scale, after):
    length = q_a.shape[0] + q_b.shape[0]
    shape = jax.ShapeDtypeStruct((length // 2, q_a.shape[1]), jnp.bfloat16)
    return simple_call(
        functools.partial(prefill_body, scale),
        (shape, shape),
        4 * length * length * q_a.shape[1],
        q_a, q_b, kv_a, kv_b, where, *after,
        specs=[VMEM] * 4 + [SMEM] + [ANY] * len(after),
    )


def strips(wide):
    tile = 1024 if wide % 1024 == 0 else wide
    return [slice(i * tile, (i + 1) * tile) for i in range(wide // tile)]


def out_body(own, other, w_own, w_other, after, *outs):
    heads = jnp.concatenate([own[...], other[...]], axis=1)
    for part in strips(w_own.shape[1]):
        w = jnp.concatenate([w_own[:, part], w_other[:, part]], axis=0)
        rows = jnp.dot(heads, w, preferred_element_type=jnp.float32)
        base = 0
        for out in outs:
            out[:, part] = rows[base : base + out.shape[0]].astype(out.dtype)
            base += out.shape[0]


def out_projection(own, other, w_own, w_other, blocks, dtype, after):
    shapes = tuple(jax.ShapeDtypeStruct((b, w_own.shape[1]), dtype) for b in blocks)
    return simple_call(
        out_body, shapes, 0, own, other, w_own, w_other, after, specs=[VMEM] * 4 + [ANY]
    )


def partial_body(tp, heads, w, kept, given):
    core = tp[0] % 2
    rows = kept.shape[0]
    for columns in strips(w.shape[1]):
        part = jnp.dot(heads[...], w[:, columns], preferred_element_type=jnp.float32)
        low, high = part[:rows], part[rows:]
        kept[:, columns] = jnp.where(core == 0, low, high).astype(kept.dtype)
        given[:, columns] = jnp.where(core == 0, high, low).astype(given.dtype)


def partial_projection(tp, heads, w):
    shape = jax.ShapeDtypeStruct((heads.shape[0] // 2, w.shape[1]), jnp.bfloat16)
    return simple_call(
        partial_body, (shape, shape), 0, tp, heads, w, specs=[SMEM, VMEM, VMEM]
    )


def add_body(a, b, *rest):
    out = rest[-1]
    out[...] = (a[...].astype(jnp.float32) + b[...].astype(jnp.float32)).astype(out.dtype)


def add(a, b, dtype, after=()):
    shape = jax.ShapeDtypeStruct(a.shape, dtype)
    specs = [VMEM] * 2 + [ANY] * len(after)
    return simple_call(add_body, shape, 0, a, b, *after, specs=specs)


def add_half_body(first, whole, part, *rest):
    out = rest[-1]
    half = part.shape[0]
    for i in range(2):
        rows = slice(i * half, (i + 1) * half)
        if i == first:
            wide = whole[rows].astype(jnp.float32) + part[...].astype(jnp.float32)
            out[rows] = wide.astype(out.dtype)
        else:
            out[rows] = whole[rows]


def add_half(first, whole, part, after):
    shape = jax.ShapeDtypeStruct(whole.shape, whole.dtype)
    specs = [VMEM] * 2 + [ANY] * len(after)
    body = functools.partial(add_half_body, first)
    return simple_call(body, shape, 0, whole, part, *after, specs=specs)


def total_body(a, b, c, d, out, token):
    token[...] = jnp.zeros(token.shape, token.dtype)
    wide = a[...].astype(jnp.float32) + b[...].astype(jnp.float32)
    wide = wide + (c[...].astype(jnp.float32) + d[...].astype(jnp.float32))
    out[...] = wide.astype(out.dtype)


def finish_body(tp, kept, taken, tokens, out):
    core = tp[0] % 2
    for i in range(out.shape[0]):
        row = 2 * i % kept.shape[0]
        first = i < out.shape[0] // 2
        held, sent = kept[row : row + 2], taken[row : row + 2]
        total = jnp.where(core == 0, held if first else sent, sent if first else held)
        out[i] = tokens[i].astype(jnp.float32) + total


def finish(tp, kept, taken, tokens):
    shape = jax.ShapeDtypeStruct(tokens.shape, jnp.float32)
    return simple_call(
        finish_body, shape, 0, tp, kept, taken, tokens,
        specs=[SMEM] + [VMEM] * 3,
    )


def shards(
    prompt_states,
    new_states,
    answer_cache,
    attn_gain,
    w_query,
    key_weight,
    value_weight,
    w_out,
    prompt_of,
    suffix_len,
):
    scale = HEAD_WIDTH ** (-0.5)
    rows = prompt_states[0, 0]
    block, width = rows.shape
    tp, grp = lax.axis_index("tp").reshape(1), lax.axis_index("grp").reshape(1)
    tp_size = lax.axis_size("tp")

    def around(value, by):
        return lax.ppermute(value, "tp", [(i, (i + 2 * by) % tp_size) for i in range(tp_size)])

    def swap(value, axis, mask):
        return lax.ppermute(value, axis, [(i, i ^ mask) for i in range(lax.axis_size(axis))])

    weights = (w_query, key_weight, value_weight)
    half = block // 2

    normed = norm_prompt(rows, attn_gain, tp, grp)
    from_down = around(normed, 1)
    from_up = around(normed, -1)
    mate_own = swap(normed, "tp", 1)

    samples, slots = new_states.shape[1], answer_cache.shape[2]
    length = block * tp_size
    fresh_normed, *fresh_tables, forth, home = prepare_fresh(
        grp, new_states[0], attn_gain, suffix_len, fixed_tables(length, slots + 8), prompt_of
    )
    fresh_q, fresh_kv, weights = fresh_qkv(fresh_normed, weights, fresh_tables)
    w_mate = swap(w_out, "tp", 1)

    where = tp
    tables = fixed_tables(0, length)
    asked = exchange_near(fresh_q, swap, ())
    from_down, from_up = hold((from_down, from_up), (asked,))
    down_top, up_low = cut(from_down, from_up)
    ahead = around(down_top, 1)
    behind = around(up_low, -1)
    near = [from_down, from_up, swap(from_down, "tp", 1), swap(from_up, "tp", 1)]
    early = qkv([normed, mate_own], weights, tables, where, 0, block)
    kept, third, fourth = exchange_pick(asked, forth, swap, (ahead, behind))
    q_a, kv_a = qkv(near, weights, tables, where, 2, block, early)
    handed_a = swap(kv_a, "role", 1)
    far = [ahead, behind, swap(ahead, "tp", 1), swap(behind, "tp", 1)]
    q_b, kv_b = qkv(far, weights, tables, where, 6, block, after=(kept,))
    handed_b = swap(kv_b, "role", 1)
    came, fourth = exchange_pass(third, fourth, swap, (kv_a,))

    heads_own, heads_other = prefill_attention(q_a, q_b, kv_a, kv_b, where, scale, (fourth,))
    heads_mate = swap(heads_other, "tp", 1)

    asked = (kept, came, swap(fourth, "grp", FOURTH))
    answered = prefix_attention(asked, handed_a, handed_b, scale, heads_own)

    sizes = (block, block, block, half, half)
    to_own, to_down, to_up, far_top, far_low = out_projection(
        heads_own, heads_mate, w_out, w_mate, sizes, jnp.bfloat16, answered
    )
    via_up = around(far_top, 1)
    via_down = around(far_low, -1)

    back = exchange_near(answered, swap, ())
    local, stats = local_attention(fresh_q, fresh_kv, answer_cache[0], suffix_len, scale, back)
    kept, third, fourth = exchange_pick(back, home, swap, (local,))
    came, fourth = exchange_pass(third, fourth, swap, ())
    up = add_half(0, to_up, via_up, (fourth,))
    down = add_half(1, to_down, via_down, (fourth,))
    back = (kept, came, swap(fourth, "grp", FOURTH))
    sum_up = around(up, 1)
    sum_down = around(down, -1)
    prefill_out, token = simple_call(
        total_body,
        (jax.ShapeDtypeStruct(rows.shape, rows.dtype), jax.ShapeDtypeStruct((8, 128), jnp.float32)),
        0, rows, to_own, sum_up, sum_down,
    )

    decoded = merge(back, local, stats, (up, down))
    kept, given = partial_projection(tp, decoded, w_out)
    level = add(kept, swap(given, "tp", 1), jnp.bfloat16)
    level = add(level, swap(level, "tp", 2), jnp.bfloat16)
    summed = add(level, swap(level, "tp", 4), jnp.float32, (token,))
    decode_out = finish(tp, summed, swap(summed, "tp", 1), new_states[0])
    return prefill_out[None, None], decode_out[None]


def solution(mesh):
    placed = (
        P("role", "grp", "tp", None),
        P("role", "grp", None, None),
        P("role", "grp", None, "tp"),
        P(),
        P(None, "tp"),
        P(None, "tp"),
        P(None, "tp"),
        P("tp", None),
        P("role", None),
        P("role", "grp"),
    )
    return jax.shard_map(
        shards,
        mesh=mesh,
        in_specs=placed,
        out_specs=(P("role", "grp", "tp", None), P("role", "grp", None, None)),
        check_vma=False,
    )
```

```python
import functools

import jax
import jax.numpy as jnp
import numpy as np
from jax import lax
from jax.experimental import pallas as pl
from jax.experimental.pallas import tpu as pltpu
from jax.sharding import PartitionSpec as P

HEAD_WIDTH = 128
EPSILON = 1e-06
ROPE_BASE = 1000000.0
VMEM_LIMIT = 14 * 1024 * 1024
WIDE_LIMIT = VMEM_LIMIT
FULL_LIMIT = VMEM_LIMIT
STEP = 900_000_000
TAIL = STEP*2
FIRST, SECOND, THIRD, FOURTH = 4, 1, 2, 8
HELD = (0, FIRST, SECOND, FIRST ^ SECOND)
SERVED = (0, THIRD, FOURTH, THIRD ^ FOURTH)


def fixed_tables(start, length):
    spans = np.concatenate([np.arange(HEAD_WIDTH // 2)] * 2)
    angles = np.arange(start, start + length)[:, None] * ROPE_BASE ** (-2.0 * spans / HEAD_WIDTH)
    sign = np.where(np.arange(HEAD_WIDTH) < HEAD_WIDTH // 2, -1.0, 1.0)
    return np.concatenate([np.cos(angles), np.sin(angles) * sign], axis=1).astype(np.float32)


VMEM = pl.BlockSpec(memory_space=pltpu.VMEM)
SMEM = pl.BlockSpec(memory_space=pltpu.SMEM)
ANY = pl.BlockSpec(memory_space=pl.ANY)
HBM = pl.BlockSpec(memory_space=pltpu.HBM)


def simple_call(body, out_shape, flops, *args, specs=None, scratch=(), limit=VMEM_LIMIT):
    nbytes = sum(a.size * a.dtype.itemsize for a in args)
    return pl.pallas_call(
        body,
        in_specs=specs or [VMEM] * len(args),
        out_specs=jax.tree.map(lambda _: VMEM, out_shape),
        out_shape=out_shape,
        scratch_shapes=list(scratch),
        compiler_params=pltpu.CompilerParams(vmem_limit_bytes=limit),
        cost_estimate=pl.CostEstimate(flops=flops, bytes_accessed=nbytes if flops > 9 * STEP else 0, transcendentals=0),
    )(*args)


def normalized(wide, gain):
    factor = lax.rsqrt(jnp.mean(wide * wide, axis=-1, keepdims=True) + EPSILON)
    return (wide * factor * gain).astype(jnp.bfloat16)


def fetch(sources, targets, sems):
    copies = [
        pltpu.make_async_copy(source, target, sems.at[i])
        for i, (source, target) in enumerate(zip(sources, targets))
    ]
    for copy in copies:
        copy.start()
    return copies


def like(*arrays):
    held = [pltpu.VMEM(a.shape, a.dtype) for a in arrays]
    return held + [pltpu.SemaphoreType.DMA((len(arrays),))]


def norm_body(tp, grp, x_far, gain_far, out, x, gain, sems):
    for copy in fetch((x_far, gain_far), (x, gain), sems):
        copy.wait()
    for i in range(x.shape[0] // 16):
        part = slice(i * 16, (i + 1) * 16)
        out[part] = normalized(x[part].astype(jnp.float32), gain[...])


def row_lengths(lengths, rows):
    samples = lengths.shape[1]
    row = lax.broadcasted_iota(jnp.int32, (rows, samples), 0)
    own = lax.broadcasted_iota(jnp.int32, (rows, samples), 1) == row // 2
    wide = jnp.where(own, lengths[...].astype(jnp.float32), 0.0)
    return jnp.sum(wide, axis=1, keepdims=True).astype(jnp.int32)


def fresh_body(samples, where, *refs):
    count = 5
    far, (out, c_out, s_out, forth, back) = refs[:count], refs[count : 2 * count]
    near, (wide, spots, sems) = refs[2 * count : 3 * count], refs[3 * count :]
    copies = fetch(far, near, sems)
    x, gain, lengths, table, prompts = near
    copies[4].wait()
    route(samples, where[0], prompts, forth, back, spots)
    for copy in copies[:4]:
        copy.wait()
    rows = out.shape[0]
    for i in range(x.shape[0]):
        wide[2 * i : 2 * i + 2] = x[i].astype(jnp.float32)
    for i in range(rows // 16):
        part = slice(i * 16, (i + 1) * 16)
        out[part] = normalized(wide[part], gain[...])
    shape = (rows, table.shape[0])
    row = lax.broadcasted_iota(jnp.int32, shape, 0)
    column = lax.broadcasted_iota(jnp.int32, shape, 1)
    at = (column == row_lengths(lengths, rows) + row % 2).astype(jnp.float32)
    both = jnp.dot(at, table[...], precision=lax.Precision.HIGHEST)
    c_out[...] = both[:, :HEAD_WIDTH]
    s_out[...] = both[:, HEAD_WIDTH:]


def prepare_fresh(grp, x, gain, lengths, table, prompts):
    samples, width = x.shape[0], x.shape[2]
    rows, wide = 2 * samples, 8 * samples
    flat = jax.ShapeDtypeStruct((rows, HEAD_WIDTH), jnp.float32)
    choice = jax.ShapeDtypeStruct((wide, wide), jnp.bfloat16)
    far = (x, gain.reshape(1, -1), lengths, jnp.asarray(table), prompts)
    *held, sems = like(*far)
    return simple_call(
        functools.partial(fresh_body, samples),
        (jax.ShapeDtypeStruct((rows, width), jnp.bfloat16), flat, flat, choice, choice),
        6 * STEP, grp, *far,
        specs=[SMEM] + [HBM] * 5,
        scratch=held
        + [
            pltpu.VMEM((rows, width), jnp.float32),
            pltpu.VMEM((2 * prompts.shape[1], wide), jnp.float32),
            sems,
        ],
    )


def norm_prompt(x, gain, tp, grp):
    shape = jax.ShapeDtypeStruct(x.shape, jnp.bfloat16)
    far = (x, gain.reshape(1, -1))
    return simple_call(
        norm_body, shape, 8 * STEP, tp, grp, *far,
        specs=[SMEM] * 2 + [HBM] * 2, scratch=like(*far), limit=FULL_LIMIT,
    )


def route(samples, grp, prompts, forth, back, spots):
    rows, count = 2 * samples, prompts.shape[1]
    wide = 2 * count
    wide_prompts = prompts[...].astype(jnp.float32)

    def grid(shape, axis):
        return lax.broadcasted_iota(jnp.int32, shape, axis)

    spread = (grid((count, wide), 1) // 2 == grid((count, wide), 0)).astype(jnp.bfloat16)
    across = jnp.dot(
        jnp.broadcast_to(wide_prompts, (8, count)).astype(jnp.bfloat16),
        spread,
        preferred_element_type=jnp.float32,
    )[:1]
    own = grid((wide, count), 1) == grid((wide, count), 0) // 2
    down = jnp.sum(jnp.where(own, wide_prompts, 0.0), axis=1, keepdims=True)
    earlier = (across == down) & (grid((wide, wide), 1) < grid((wide, wide), 0))
    rank = jnp.sum(earlier.astype(jnp.float32), axis=1, keepdims=True)
    spots[...] = jnp.broadcast_to(down * rows + rank, spots.shape)

    def cells(masks):
        parts = [spots[pl.ds(pl.multiple_of((grp ^ m) * rows, rows), rows)] for m in masks]
        return jnp.concatenate(parts, axis=0)

    def names(masks):
        column = grid((1, 4 * rows), 1)
        start = jnp.zeros((1, 4 * rows), jnp.int32)
        for i, m in enumerate(masks):
            start = jnp.where(column // rows == i, (grp ^ m) * rows, start)
        return (start + column % rows).astype(jnp.float32)

    picked = (cells(HELD) == names(SERVED)).astype(jnp.float32)
    forth[...] = picked.T.astype(jnp.bfloat16)
    back[...] = (cells(SERVED) == names(HELD)).astype(jnp.bfloat16)


def hold(values, after):
    count = len(values)
    return pl.pallas_call(
        lambda *refs: None,
        in_specs=[ANY] * (count + len(after)),
        out_specs=[ANY] * count,
        out_shape=[jax.ShapeDtypeStruct(v.shape, v.dtype) for v in values],
        input_output_aliases={i: i for i in range(count)},
        compiler_params=pltpu.CompilerParams(vmem_limit_bytes=VMEM_LIMIT),
        cost_estimate=pl.CostEstimate(flops=0, bytes_accessed=0, transcendentals=0),
    )(*values, *after)


def join_body(a, b, *rest):
    out = rest[-1]
    out[: a.shape[0]] = a[...]
    out[a.shape[0] :] = b[...]


def pick_body(choice, near, far, *rest):
    kept, third, fourth = rest[-3:]
    rows = kept.shape[0]
    held = jnp.concatenate([near[...], far[...]], axis=0)
    picked = jnp.dot(choice[...], held, preferred_element_type=jnp.float32).astype(jnp.bfloat16)
    kept[...] = picked[:rows]
    third[:rows] = picked[rows : 2 * rows]
    third[rows:] = picked[3 * rows :]
    fourth[...] = picked[2 * rows : 3 * rows]


def pass_body(part, came, *rest):
    out = rest[-1]
    rows = part.shape[0]
    out[...] = part[...] + came[rows:]


def exchange_near(value, swap, after, cost=0):
    shape = jax.ShapeDtypeStruct((2 * value.shape[0], value.shape[1]), value.dtype)
    args = (value, swap(value, "grp", FIRST))
    specs = [VMEM] * 2 + [ANY] * len(after)
    return simple_call(join_body, shape, cost, *args, *after, specs=specs)


def exchange_pick(near, choice, swap, after, cost=0):
    rows, wide = near.shape[0] // 2, near.shape[1]
    shape = lambda n: jax.ShapeDtypeStruct((n * rows, wide), near.dtype)
    args = (choice, near, swap(near, "grp", SECOND))
    return simple_call(
        pick_body, (shape(1), shape(2), shape(1)), cost, *args, *after,
        specs=[VMEM] * 3 + [ANY] * len(after),
    )


def exchange_pass(third, fourth, swap, after, cost=0):
    came = swap(third, "grp", THIRD)
    shape = jax.ShapeDtypeStruct(fourth.shape, fourth.dtype)
    specs = [VMEM] * 2 + [ANY] * len(after)
    return came, simple_call(pass_body, shape, cost, fourth, came, *after, specs=specs)


def arrived(kept, came, last):
    return kept[...] + came[: kept.shape[0]] + last[...]


def cut_body(a, b, top, low):
    half = top.shape[0]
    top[...] = a[:half]
    low[...] = b[half:]


def cut(a, b):
    shape = jax.ShapeDtypeStruct((a.shape[0] // 2, a.shape[1]), a.dtype)
    return simple_call(cut_body, (shape, shape), 0, a, b)


TURNS = (0, 0, -1, 1, -1, 1, 2, 2)
FLIPS = (0, 1, 0, 0, 1, 1, 0, 1)


def start_of(tp, chips, block, i):
    chip = lax.rem(tp // 2 + TURNS[i] + chips, chips)
    return (2 * chip + ((tp % 2) ^ FLIPS[i])) * block


def rotate(acc, c, s, q_out, kv_out, base):
    wide = q_out.shape[1]
    for h in range(wide // HEAD_WIDTH + 1):
        v = acc[:, h * HEAD_WIDTH : (h + 1) * HEAD_WIDTH]
        v = (v * c + pltpu.roll(v, HEAD_WIDTH // 2, 1) * s).astype(jnp.bfloat16)
        if h * HEAD_WIDTH == wide:
            kv_out[base:, :HEAD_WIDTH] = v
        else:
            q_out[base:, h * HEAD_WIDTH : (h + 1) * HEAD_WIDTH] = v
    kv_out[base:, HEAD_WIDTH:] = acc[:, wide + HEAD_WIDTH :].astype(jnp.bfloat16)


def chunks(depth):
    count = 5 if depth % 640 == 0 else 1
    return [slice(i * depth // count, (i + 1) * depth // count) for i in range(count)]


def fresh_qkv_body(x, wq, wk, wv, cos, sin, q_out, kv_out, joined, acc):
    for i, part in enumerate(chunks(x.shape[1])):
        w = jnp.concatenate([wq[part], wk[part], wv[part]], axis=1)
        joined[part] = w
        piece = jnp.dot(x[:, part], w, preferred_element_type=jnp.float32)
        acc[...] = piece if i == 0 else acc[...] + piece
    rotate(acc, cos[...], sin[...], q_out, kv_out, 0)


def fresh_qkv(x, weights, tables):
    rows, depth = x.shape
    total = sum(w.shape[1] for w in weights)
    shape = lambda *dims: jax.ShapeDtypeStruct(dims, jnp.bfloat16)
    return simple_call(
        fresh_qkv_body,
        (shape(rows, total - 2 * HEAD_WIDTH), shape(rows, 2 * HEAD_WIDTH), shape(depth, total)),
        STEP, x, *weights, *tables,
        scratch=[pltpu.VMEM((rows, total), jnp.float32)],
    )


def qkv_body(n, first, block, early, skip, *refs):
    xs, (w, table, where, *rest) = refs[:n], refs[n:]
    q_out, kv_out, acc = rest[-3:]
    for i, part in enumerate(chunks(w.shape[0])):
        x = jnp.concatenate([r[:, part] for r in xs], axis=0)
        piece = jnp.dot(x, w[part], preferred_element_type=jnp.float32)
        acc[...] = piece if i == 0 else acc[...] + piece
    base = 0
    if early:
        q_early, kv_early = rest[:2]
        base = q_early.shape[0]
        q_out[:base] = q_early[...]
        kv_out[:base] = kv_early[...]
    chips = table.shape[0] // block // 2
    spots = [start_of(where[0], chips, block, first + i) for i in range(acc.shape[0] // block)]
    spots = [pl.ds(pl.multiple_of(spot, block), block) for spot in spots]
    both = jnp.concatenate([table[spot] for spot in spots], axis=0)
    rotate(acc, both[:, :HEAD_WIDTH], both[:, HEAD_WIDTH:], q_out, kv_out, base)


def qkv(blocks, joined, table, where, first, block, cost, early=(), after=()):
    rows, (depth, total) = sum(b.shape[0] for b in blocks), joined.shape
    base = early[0].shape[0] if early else 0
    shape = lambda wide: jax.ShapeDtypeStruct((base + rows, wide), jnp.bfloat16)
    return simple_call(
        functools.partial(qkv_body, len(blocks), first, block, bool(early), len(after)),
        (shape(total - 2 * HEAD_WIDTH), shape(2 * HEAD_WIDTH)),
        cost, *blocks, joined, jnp.asarray(table), where, *early, *after,
        specs=[VMEM] * (len(blocks) + 2) + [SMEM] + [VMEM] * len(early) + [ANY] * len(after),
        scratch=[pltpu.VMEM((rows, total), jnp.float32)],
    )


def dot_t(a, b):
    return lax.dot_general(a, b, (((1,), (1,)), ((), ())), preferred_element_type=jnp.float32)


def local_body(scale, q, kv, cache_far, lengths_far, after, out, stats, cache, lengths, sems):
    copies = fetch((cache_far, lengths_far), (cache, lengths), sems)
    for copy in copies:
        copy.wait()
    width, rows = HEAD_WIDTH, q.shape[0]
    groups, samples = q.shape[1] // width, cache.shape[0]
    slots = cache.shape[1]
    query = jnp.concatenate(
        [q[:, g * width : (g + 1) * width] for g in range(groups)], axis=0
    )
    old = cache[...].reshape(samples * slots, 2 * width)
    total = groups * rows
    row = lax.broadcasted_iota(jnp.int32, (total, 1), 0) % rows
    column = lax.broadcasted_iota(jnp.int32, (1, samples * slots), 1)
    score_old = dot_t(query, old[:, :width]) * scale
    limit = row // 2 * slots + jnp.concatenate([row_lengths(lengths, rows)] * groups, axis=0)
    allowed = (column >= row // 2 * slots) & (column < limit)
    score_old = jnp.where(allowed, score_old, -jnp.inf)
    fresh = lax.broadcasted_iota(jnp.int32, (1, rows), 1)
    score_new = dot_t(query, kv[:, :width]) * scale
    score_new = jnp.where((fresh // 2 == row // 2) & (fresh <= row), score_new, -jnp.inf)
    peak = jnp.maximum(
        jnp.max(score_old, axis=1, keepdims=True), jnp.max(score_new, axis=1, keepdims=True)
    )
    expo_old, expo_new = jnp.exp(score_old - peak), jnp.exp(score_new - peak)
    both = jnp.sum(expo_old, axis=1, keepdims=True) + jnp.sum(expo_new, axis=1, keepdims=True)
    mixed = jnp.dot(
        expo_old.astype(jnp.bfloat16), old[:, width:], preferred_element_type=jnp.float32
    ) + jnp.dot(
        expo_new.astype(jnp.bfloat16), kv[:, width:], preferred_element_type=jnp.float32
    )
    out[...] = mixed
    lane = lax.broadcasted_iota(jnp.int32, stats.shape, 1)
    stats[...] = jnp.where(lane == 0, peak, both)


def local_attention(q, kv, cache, lengths, scale, after):
    total = q.shape[1] // HEAD_WIDTH * q.shape[0]
    shape = jax.ShapeDtypeStruct((total, HEAD_WIDTH), jnp.float32)
    flops = 4 * total * cache.shape[0] * cache.shape[1] * HEAD_WIDTH
    return simple_call(
        functools.partial(local_body, scale), (shape, shape), flops,
        q, kv, cache, lengths, after,
        specs=[VMEM] * 2 + [HBM] * 2 + [ANY], scratch=like(cache, lengths),
    )


def prefix_body(scale, kept, came, last, kv_a, kv_b, after, out):
    width, rows = HEAD_WIDTH, kept.shape[0]
    groups = kept.shape[1] // width
    picked = arrived(kept, came, last)
    query = jnp.concatenate([picked[:, g * width : (g + 1) * width] for g in range(groups)], axis=0)
    pairs = jnp.concatenate([kv_a[...], kv_b[...]], axis=0)
    score = dot_t(query, pairs[:, :width]) * scale
    peak = jnp.max(score, axis=1, keepdims=True)
    expo = jnp.exp(score - peak)
    both = jnp.sum(expo, axis=1, keepdims=True)
    mixed = jnp.dot(expo.astype(jnp.bfloat16), pairs[:, width:], preferred_element_type=jnp.float32)
    mixed = (mixed / both).astype(jnp.bfloat16)
    level = peak + jnp.log(both)
    lane = lax.broadcasted_iota(jnp.int32, (rows, width), 1)
    tail = jnp.zeros((rows, width), jnp.bfloat16)
    for g in range(groups):
        out[:, g * width : (g + 1) * width] = mixed[g * rows : (g + 1) * rows]
        rest = level[g * rows : (g + 1) * rows]
        for part in range(3):
            high = rest.astype(jnp.bfloat16)
            rest = rest - high.astype(jnp.float32)
            tail = jnp.where(lane == g * 3 + part, high, tail)
    out[:, groups * width :] = tail


def prefix_attention(asked, kv_a, kv_b, scale, after):
    rows, wide = asked[0].shape
    shape = jax.ShapeDtypeStruct((rows, wide + HEAD_WIDTH), jnp.bfloat16)
    return simple_call(
        functools.partial(prefix_body, scale), shape, 4 * STEP, *asked, kv_a, kv_b, after,
        specs=[VMEM] * 5 + [ANY],
    )


def merge_body(kept, came, last, local, stats, *rest):
    out = rest[-1]
    width, rows = HEAD_WIDTH, kept.shape[0]
    groups = local.shape[0] // rows
    picked = arrived(kept, came, last).astype(jnp.float32)
    tail = picked[:, groups * width :]
    for g in range(groups):
        level = tail[:, g * 3 : g * 3 + 1] + tail[:, g * 3 + 1 : g * 3 + 2]
        level = level + tail[:, g * 3 + 2 : g * 3 + 3]
        peak = stats[g * rows : (g + 1) * rows, 0:1]
        both = stats[g * rows : (g + 1) * rows, 1:2]
        top = jnp.maximum(level, peak)
        factor_pre, factor_loc = jnp.exp(level - top), jnp.exp(peak - top)
        total = factor_pre + both * factor_loc
        mixed = picked[:, g * width : (g + 1) * width] * factor_pre
        mixed = mixed + local[g * rows : (g + 1) * rows] * factor_loc
        out[:, g * width : (g + 1) * width] = (mixed / total).astype(jnp.bfloat16)


def merge(back, local, stats, after):
    rows, wide = back[0].shape
    shape = jax.ShapeDtypeStruct((rows, wide - HEAD_WIDTH), jnp.bfloat16)
    return simple_call(
        merge_body, shape, 0, *back, local, stats, *after,
        specs=[VMEM] * 5 + [ANY] * len(after),
    )


def prefill_body(scale, q_a, q_b, kv_a, kv_b, where, *rest):
    own, other = rest[-2:]
    width = HEAD_WIDTH
    groups = q_a.shape[1] // width
    block = own.shape[0] // 4
    pairs = jnp.concatenate([kv_a[...], kv_b[...]], axis=0)
    length = pairs.shape[0]

    def places(shape, axis):
        spot = lax.broadcasted_iota(jnp.int32, shape, axis)
        shift = jnp.zeros(shape, jnp.int32)
        count = length // block
        for i in range(count):
            start = start_of(where[0], count // 2, block, i)
            shift = jnp.where(spot // block == i, start - i * block, shift)
        return spot + shift

    allowed = places((length, 1), 0) >= places((1, length), 1)
    for g in range(groups):
        cols = slice(g * width, (g + 1) * width)
        query = jnp.concatenate([q_a[:, cols], q_b[:, cols]], axis=0)
        score = jnp.where(allowed, dot_t(query, pairs[:, :width]) * scale, -jnp.inf)
        expo = jnp.exp(score - jnp.max(score, axis=1, keepdims=True))
        both = jnp.sum(expo, axis=1, keepdims=True)
        mixed = jnp.dot(
            expo.astype(jnp.bfloat16), pairs[:, width:], preferred_element_type=jnp.float32
        )
        mixed = (mixed / both).astype(jnp.bfloat16)
        part = lambda i, n: mixed[i * block : (i + n) * block]
        for out, at in ((own, (0, 2, 6)), (other, (1, 4, 7))):
            out[:block, cols] = part(at[0], 1)
            out[block : 3 * block, cols] = part(at[1], 2)
            out[3 * block :, cols] = part(at[2], 1)


def prefill_attention(q_a, q_b, kv_a, kv_b, where, scale, after):
    length = q_a.shape[0] + q_b.shape[0]
    shape = jax.ShapeDtypeStruct((length // 2, q_a.shape[1]), jnp.bfloat16)
    return simple_call(
        functools.partial(prefill_body, scale),
        (shape, shape),
        4 * length * length * q_a.shape[1],
        q_a, q_b, kv_a, kv_b, where, *after,
        specs=[VMEM] * 4 + [SMEM] + [ANY] * len(after),
    )


def strips(wide):
    tile = 1024 if wide % 1024 == 0 else wide
    return [slice(i * tile, (i + 1) * tile) for i in range(wide // tile)]


def stage_body(own, other, *rest):
    both, sems = rest[-2:]
    depth = own.shape[0]
    copies = [
        pltpu.make_async_copy(own, both.at[:depth], sems.at[0]),
        pltpu.make_async_copy(other, both.at[depth:], sems.at[1]),
    ]
    for copy in copies:
        copy.start()
    for copy in copies:
        copy.wait()


def stage(own, other, after):
    shape = jax.ShapeDtypeStruct((2 * own.shape[0], own.shape[1]), own.dtype)
    return simple_call(
        stage_body, shape, 0, own, other, *after,
        specs=[HBM] * 2 + [ANY] * len(after), scratch=[pltpu.SemaphoreType.DMA((2,))],
    )


def out_body(own, other, w, *rest):
    outs = rest[1:]
    heads = jnp.concatenate([own[...], other[...]], axis=1)
    for part in strips(w.shape[1]):
        rows = jnp.dot(heads, w[:, part], preferred_element_type=jnp.float32)
        base = 0
        for out in outs:
            out[:, part] = rows[base : base + out.shape[0]].astype(out.dtype)
            base += out.shape[0]


def out_projection(own, other, w, blocks, dtype, after):
    shapes = tuple(jax.ShapeDtypeStruct((b, w.shape[1]), dtype) for b in blocks)
    return simple_call(
        out_body, shapes, 0, own, other, w, after, specs=[VMEM] * 3 + [ANY]
    )


def partial_body(tp, heads, w, kept, given):
    core = tp[0] % 2
    rows, depth = kept.shape[0], heads.shape[1]
    for columns in strips(w.shape[1]):
        part = jnp.dot(heads[...], w[:depth, columns], preferred_element_type=jnp.float32)
        low, high = part[:rows], part[rows:]
        kept[:, columns] = jnp.where(core == 0, low, high).astype(kept.dtype)
        given[:, columns] = jnp.where(core == 0, high, low).astype(given.dtype)


def partial_projection(tp, heads, w):
    shape = jax.ShapeDtypeStruct((heads.shape[0] // 2, w.shape[1]), jnp.bfloat16)
    return simple_call(
        partial_body, (shape, shape), TAIL, tp, heads, w, specs=[SMEM, VMEM, VMEM]
    )


def add_body(a, b, *rest):
    out = rest[-1]
    out[...] = (a[...].astype(jnp.float32) + b[...].astype(jnp.float32)).astype(out.dtype)


def add(a, b, dtype, after=()):
    shape = jax.ShapeDtypeStruct(a.shape, dtype)
    specs = [VMEM] * 2 + [ANY] * len(after)
    return simple_call(add_body, shape, TAIL, a, b, *after, specs=specs)


def add_four_body(own, far, down, up, *rest):
    out = rest[-1]
    wide = own[...].astype(jnp.float32) + far[...].astype(jnp.float32)
    out[...] = wide + (down[...].astype(jnp.float32) + up[...].astype(jnp.float32))


def add_four(own, far, down, up, after):
    shape = jax.ShapeDtypeStruct(own.shape, jnp.float32)
    specs = [VMEM] * 4 + [ANY] * len(after)
    return simple_call(add_four_body, shape, TAIL, own, far, down, up, *after, specs=specs)


def add_half_body(first, whole, part, *rest):
    out = rest[-1]
    half = part.shape[0]
    for i in range(2):
        rows = slice(i * half, (i + 1) * half)
        if i == first:
            wide = whole[rows].astype(jnp.float32) + part[...].astype(jnp.float32)
            out[rows] = wide.astype(out.dtype)
        else:
            out[rows] = whole[rows]


def add_half(first, whole, part, after):
    shape = jax.ShapeDtypeStruct(whole.shape, whole.dtype)
    specs = [VMEM] * 2 + [ANY] * len(after)
    body = functools.partial(add_half_body, first)
    return simple_call(body, shape, 0, whole, part, *after, specs=specs)


def total_body(a, b, c, d, out, token):
    token[...] = jnp.zeros(token.shape, token.dtype)
    wide = a[...].astype(jnp.float32) + b[...].astype(jnp.float32)
    wide = wide + (c[...].astype(jnp.float32) + d[...].astype(jnp.float32))
    out[...] = wide.astype(out.dtype)


def finish_body(tp, kept, taken, tokens, out):
    core = tp[0] % 2
    for i in range(out.shape[0]):
        row = 2 * i % kept.shape[0]
        first = i < out.shape[0] // 2
        held, sent = kept[row : row + 2], taken[row : row + 2]
        total = jnp.where(core == 0, held if first else sent, sent if first else held)
        out[i] = tokens[i].astype(jnp.float32) + total


def finish(tp, kept, taken, tokens):
    shape = jax.ShapeDtypeStruct(tokens.shape, jnp.float32)
    return simple_call(
        finish_body, shape, TAIL, tp, kept, taken, tokens,
        specs=[SMEM] + [VMEM] * 3,
    )


def shards(
    prompt_states,
    new_states,
    answer_cache,
    attn_gain,
    w_query,
    key_weight,
    value_weight,
    w_out,
    prompt_of,
    suffix_len,
):
    scale = HEAD_WIDTH ** (-0.5)
    rows = prompt_states[0, 0]
    block, width = rows.shape
    tp, grp = lax.axis_index("tp").reshape(1), lax.axis_index("grp").reshape(1)
    tp_size = lax.axis_size("tp")

    def around(value, by):
        return lax.ppermute(value, "tp", [(i, (i + 2 * by) % tp_size) for i in range(tp_size)])

    def swap(value, axis, mask):
        return lax.ppermute(value, axis, [(i, i ^ mask) for i in range(lax.axis_size(axis))])

    weights = (w_query, key_weight, value_weight)
    half = block // 2

    normed = norm_prompt(rows, attn_gain, tp, grp)
    from_down = around(normed, 1)
    from_up = around(normed, -1)
    mate_own = swap(normed, "tp", 1)

    samples, slots = new_states.shape[1], answer_cache.shape[2]
    length = block * tp_size
    fresh_normed, *fresh_tables, forth, home = prepare_fresh(
        grp, new_states[0], attn_gain, suffix_len, fixed_tables(length, slots + 8), prompt_of
    )
    fresh_q, fresh_kv, weights = fresh_qkv(fresh_normed, weights, fresh_tables)
    w_mate = swap(w_out, "tp", 1)

    where = tp
    tables = fixed_tables(0, length)
    asked = exchange_near(fresh_q, swap, ())
    early = qkv([normed, mate_own], weights, tables, where, 0, block, STEP)
    kept, third, fourth = exchange_pick(asked, forth, swap, ())
    from_down, from_up = hold((from_down, from_up), (third, early[1]))
    down_top, up_low = cut(from_down, from_up)
    ahead = around(down_top, 1)
    behind = around(up_low, -1)
    near = [from_down, from_up, swap(from_down, "tp", 1), swap(from_up, "tp", 1)]
    q_a, kv_a = qkv(near, weights, tables, where, 2, block, 0, early)
    handed_a = swap(kv_a, "role", 1)
    w_both = stage(w_out, w_mate, (kv_a,))
    came, fourth = exchange_pass(third, fourth, swap, ())
    ahead, behind = hold((ahead, behind), (w_both,))
    last = swap(fourth, "grp", FOURTH)
    far = [ahead, behind, swap(ahead, "tp", 1), swap(behind, "tp", 1)]
    q_b, kv_b = qkv(far, weights, tables, where, 6, block, 0)
    handed_b = swap(kv_b, "role", 1)

    heads_own, heads_other = prefill_attention(q_a, q_b, kv_a, kv_b, where, scale, ())
    heads_mate = swap(heads_other, "tp", 1)

    asked = (kept, came, last)
    answered = prefix_attention(asked, handed_a, handed_b, scale, heads_own)

    sizes = (block, block, block, half, half)
    to_own, to_down, to_up, far_top, far_low = out_projection(
        heads_own, heads_mate, w_both, sizes, jnp.bfloat16, answered
    )
    via_up = around(far_top, 1)
    via_down = around(far_low, -1)

    back = exchange_near(answered, swap, (), STEP)
    local, stats = local_attention(fresh_q, fresh_kv, answer_cache[0], suffix_len, scale, back)
    kept, third, fourth = exchange_pick(back, home, swap, (local,), STEP)
    came, fourth = exchange_pass(third, fourth, swap, (), STEP)
    up = add_half(0, to_up, via_up, (fourth,))
    down = add_half(1, to_down, via_down, (fourth,))
    back = (kept, came, swap(fourth, "grp", FOURTH))
    sum_up = around(up, 1)
    sum_down = around(down, -1)
    prefill_out, token = simple_call(
        total_body,
        (jax.ShapeDtypeStruct(rows.shape, rows.dtype), jax.ShapeDtypeStruct((8, 128), jnp.float32)),
        0, rows, to_own, sum_up, sum_down,
    )

    decoded = merge(back, local, stats, (up, down))
    kept, given = partial_projection(tp, decoded, w_both)
    level = add(kept, swap(given, "tp", 1), jnp.bfloat16)
    summed = add_four(level, around(level, 2), around(level, 1), around(level, -1), (token,))
    decode_out = finish(tp, summed, swap(summed, "tp", 1), new_states[0])
    return prefill_out[None, None], decode_out[None]


def solution(mesh):
    placed = (
        P("role", "grp", "tp", None),
        P("role", "grp", None, None),
        P("role", "grp", None, "tp"),
        P(),
        P(None, "tp"),
        P(None, "tp"),
        P(None, "tp"),
        P("tp", None),
        P("role", None),
        P("role", "grp"),
    )
    return jax.shard_map(
        shards,
        mesh=mesh,
        in_specs=placed,
        out_specs=(P("role", "grp", "tp", None), P("role", "grp", None, None)),
        check_vma=False,
    )
```

```python
import functools

import jax
import jax.numpy as jnp
import numpy as np
from jax import lax
from jax.experimental import pallas as pl
from jax.experimental.pallas import tpu as pltpu
from jax.sharding import PartitionSpec as P

HEAD_WIDTH = 128
EPSILON = 1e-06
ROPE_BASE = 1000000.0
VMEM_LIMIT = 14 * 1024 * 1024
WIDE_LIMIT = VMEM_LIMIT
FULL_LIMIT = VMEM_LIMIT
STEP = 900_000_000
TAIL = STEP*2
FIRST, SECOND, THIRD, FOURTH = 4, 1, 2, 8
HELD = (0, FIRST, SECOND, FIRST ^ SECOND)
SERVED = (0, THIRD, FOURTH, THIRD ^ FOURTH)


def fixed_tables(start, length):
    spans = np.concatenate([np.arange(HEAD_WIDTH // 2)] * 2)
    angles = np.arange(start, start + length)[:, None] * ROPE_BASE ** (-2.0 * spans / HEAD_WIDTH)
    sign = np.where(np.arange(HEAD_WIDTH) < HEAD_WIDTH // 2, -1.0, 1.0)
    return np.concatenate([np.cos(angles), np.sin(angles) * sign], axis=1).astype(np.float32)


VMEM = pl.BlockSpec(memory_space=pltpu.VMEM)
SMEM = pl.BlockSpec(memory_space=pltpu.SMEM)
ANY = pl.BlockSpec(memory_space=pl.ANY)
HBM = pl.BlockSpec(memory_space=pltpu.HBM)


def simple_call(body, out_shape, flops, *args, specs=None, scratch=(), limit=VMEM_LIMIT):
    nbytes = sum(a.size * a.dtype.itemsize for a in args)
    return pl.pallas_call(
        body,
        in_specs=specs or [VMEM] * len(args),
        out_specs=jax.tree.map(lambda _: VMEM, out_shape),
        out_shape=out_shape,
        scratch_shapes=list(scratch),
        compiler_params=pltpu.CompilerParams(vmem_limit_bytes=limit),
        cost_estimate=pl.CostEstimate(flops=flops, bytes_accessed=nbytes if flops > 9 * STEP else 0, transcendentals=0),
    )(*args)


def normalized(wide, gain):
    factor = lax.rsqrt(jnp.mean(wide * wide, axis=-1, keepdims=True) + EPSILON)
    return (wide * factor * gain).astype(jnp.bfloat16)


def fetch(sources, targets, sems):
    copies = [
        pltpu.make_async_copy(source, target, sems.at[i])
        for i, (source, target) in enumerate(zip(sources, targets))
    ]
    for copy in copies:
        copy.start()
    return copies


def like(*arrays):
    held = [pltpu.VMEM(a.shape, a.dtype) for a in arrays]
    return held + [pltpu.SemaphoreType.DMA((len(arrays),))]


def norm_body(tp, grp, x_far, gain_far, out, x, gain, sems):
    for copy in fetch((x_far, gain_far), (x, gain), sems):
        copy.wait()
    for i in range(x.shape[0] // 16):
        part = slice(i * 16, (i + 1) * 16)
        out[part] = normalized(x[part].astype(jnp.float32), gain[...])


def row_lengths(lengths, rows):
    samples = lengths.shape[1]
    row = lax.broadcasted_iota(jnp.int32, (rows, samples), 0)
    own = lax.broadcasted_iota(jnp.int32, (rows, samples), 1) == row // 2
    wide = jnp.where(own, lengths[...].astype(jnp.float32), 0.0)
    return jnp.sum(wide, axis=1, keepdims=True).astype(jnp.int32)


def fresh_body(samples, where, *refs):
    count = 5
    far, (out, c_out, s_out, forth, back) = refs[:count], refs[count : 2 * count]
    near, (wide, spots, sems) = refs[2 * count : 3 * count], refs[3 * count :]
    copies = fetch(far, near, sems)
    x, gain, lengths, table, prompts = near
    copies[4].wait()
    route(samples, where[0], prompts, forth, back, spots)
    for copy in copies[:4]:
        copy.wait()
    rows = out.shape[0]
    for i in range(x.shape[0]):
        wide[2 * i : 2 * i + 2] = x[i].astype(jnp.float32)
    for i in range(rows // 16):
        part = slice(i * 16, (i + 1) * 16)
        out[part] = normalized(wide[part], gain[...])
    shape = (rows, table.shape[0])
    row = lax.broadcasted_iota(jnp.int32, shape, 0)
    column = lax.broadcasted_iota(jnp.int32, shape, 1)
    at = (column == row_lengths(lengths, rows) + row % 2).astype(jnp.float32)
    both = jnp.dot(at, table[...], precision=lax.Precision.HIGHEST)
    c_out[...] = both[:, :HEAD_WIDTH]
    s_out[...] = both[:, HEAD_WIDTH:]


def prepare_fresh(grp, x, gain, lengths, table, prompts):
    samples, width = x.shape[0], x.shape[2]
    rows, wide = 2 * samples, 8 * samples
    flat = jax.ShapeDtypeStruct((rows, HEAD_WIDTH), jnp.float32)
    choice = jax.ShapeDtypeStruct((wide, wide), jnp.bfloat16)
    far = (x, gain.reshape(1, -1), lengths, jnp.asarray(table), prompts)
    *held, sems = like(*far)
    return simple_call(
        functools.partial(fresh_body, samples),
        (jax.ShapeDtypeStruct((rows, width), jnp.bfloat16), flat, flat, choice, choice),
        6 * STEP, grp, *far,
        specs=[SMEM] + [HBM] * 5,
        scratch=held
        + [
            pltpu.VMEM((rows, width), jnp.float32),
            pltpu.VMEM((2 * prompts.shape[1], wide), jnp.float32),
            sems,
        ],
    )


def norm_prompt(x, gain, tp, grp):
    shape = jax.ShapeDtypeStruct(x.shape, jnp.bfloat16)
    far = (x, gain.reshape(1, -1))
    return simple_call(
        norm_body, shape, 8 * STEP, tp, grp, *far,
        specs=[SMEM] * 2 + [HBM] * 2, scratch=like(*far), limit=FULL_LIMIT,
    )


def route(samples, grp, prompts, forth, back, spots):
    rows, count = 2 * samples, prompts.shape[1]
    wide = 2 * count
    wide_prompts = prompts[...].astype(jnp.float32)

    def grid(shape, axis):
        return lax.broadcasted_iota(jnp.int32, shape, axis)

    spread = (grid((count, wide), 1) // 2 == grid((count, wide), 0)).astype(jnp.bfloat16)
    across = jnp.dot(
        jnp.broadcast_to(wide_prompts, (8, count)).astype(jnp.bfloat16),
        spread,
        preferred_element_type=jnp.float32,
    )[:1]
    own = grid((wide, count), 1) == grid((wide, count), 0) // 2
    down = jnp.sum(jnp.where(own, wide_prompts, 0.0), axis=1, keepdims=True)
    earlier = (across == down) & (grid((wide, wide), 1) < grid((wide, wide), 0))
    rank = jnp.sum(earlier.astype(jnp.float32), axis=1, keepdims=True)
    spots[...] = jnp.broadcast_to(down * rows + rank, spots.shape)

    def cells(masks):
        parts = [spots[pl.ds(pl.multiple_of((grp ^ m) * rows, rows), rows)] for m in masks]
        return jnp.concatenate(parts, axis=0)

    def names(masks):
        column = grid((1, 4 * rows), 1)
        start = jnp.zeros((1, 4 * rows), jnp.int32)
        for i, m in enumerate(masks):
            start = jnp.where(column // rows == i, (grp ^ m) * rows, start)
        return (start + column % rows).astype(jnp.float32)

    picked = (cells(HELD) == names(SERVED)).astype(jnp.float32)
    forth[...] = picked.T.astype(jnp.bfloat16)
    back[...] = (cells(SERVED) == names(HELD)).astype(jnp.bfloat16)


def hold(values, after):
    count = len(values)
    return pl.pallas_call(
        lambda *refs: None,
        in_specs=[ANY] * (count + len(after)),
        out_specs=[ANY] * count,
        out_shape=[jax.ShapeDtypeStruct(v.shape, v.dtype) for v in values],
        input_output_aliases={i: i for i in range(count)},
        compiler_params=pltpu.CompilerParams(vmem_limit_bytes=VMEM_LIMIT),
        cost_estimate=pl.CostEstimate(flops=0, bytes_accessed=0, transcendentals=0),
    )(*values, *after)


def join_body(a, b, *rest):
    out = rest[-1]
    out[: a.shape[0]] = a[...]
    out[a.shape[0] :] = b[...]


def pick_body(choice, near, far, *rest):
    kept, third, fourth = rest[-3:]
    rows = kept.shape[0]
    held = jnp.concatenate([near[...], far[...]], axis=0)
    picked = jnp.dot(choice[...], held, preferred_element_type=jnp.float32).astype(jnp.bfloat16)
    kept[...] = picked[:rows]
    third[:rows] = picked[rows : 2 * rows]
    third[rows:] = picked[3 * rows :]
    fourth[...] = picked[2 * rows : 3 * rows]


def pass_body(part, came, *rest):
    out = rest[-1]
    rows = part.shape[0]
    out[...] = part[...] + came[rows:]


def exchange_near(value, swap, after, cost=0):
    shape = jax.ShapeDtypeStruct((2 * value.shape[0], value.shape[1]), value.dtype)
    args = (value, swap(value, "grp", FIRST))
    specs = [VMEM] * 2 + [ANY] * len(after)
    return simple_call(join_body, shape, cost, *args, *after, specs=specs)


def exchange_pick(near, choice, swap, after, cost=0):
    rows, wide = near.shape[0] // 2, near.shape[1]
    shape = lambda n: jax.ShapeDtypeStruct((n * rows, wide), near.dtype)
    args = (choice, near, swap(near, "grp", SECOND))
    return simple_call(
        pick_body, (shape(1), shape(2), shape(1)), cost, *args, *after,
        specs=[VMEM] * 3 + [ANY] * len(after),
    )


def exchange_pass(third, fourth, swap, after, cost=0):
    came = swap(third, "grp", THIRD)
    shape = jax.ShapeDtypeStruct(fourth.shape, fourth.dtype)
    specs = [VMEM] * 2 + [ANY] * len(after)
    return came, simple_call(pass_body, shape, cost, fourth, came, *after, specs=specs)


def arrived(kept, came, last):
    return kept[...] + came[: kept.shape[0]] + last[...]


def cut_body(a, b, top, low):
    half = top.shape[0]
    top[...] = a[:half]
    low[...] = b[half:]


def cut(a, b):
    shape = jax.ShapeDtypeStruct((a.shape[0] // 2, a.shape[1]), a.dtype)
    return simple_call(cut_body, (shape, shape), 0, a, b)


TURNS = (0, 0, -1, 1, -1, 1, 2, 2)
FLIPS = (0, 1, 0, 0, 1, 1, 0, 1)


def start_of(tp, chips, block, i):
    chip = lax.rem(tp // 2 + TURNS[i] + chips, chips)
    return (2 * chip + ((tp % 2) ^ FLIPS[i])) * block


def rotate(acc, c, s, q_out, kv_out, base):
    wide = q_out.shape[1]
    for h in range(wide // HEAD_WIDTH + 1):
        v = acc[:, h * HEAD_WIDTH : (h + 1) * HEAD_WIDTH]
        v = (v * c + pltpu.roll(v, HEAD_WIDTH // 2, 1) * s).astype(jnp.bfloat16)
        if h * HEAD_WIDTH == wide:
            kv_out[base:, :HEAD_WIDTH] = v
        else:
            q_out[base:, h * HEAD_WIDTH : (h + 1) * HEAD_WIDTH] = v
    kv_out[base:, HEAD_WIDTH:] = acc[:, wide + HEAD_WIDTH :].astype(jnp.bfloat16)


def chunks(depth):
    count = 5 if depth % 640 == 0 else 1
    return [slice(i * depth // count, (i + 1) * depth // count) for i in range(count)]


def fresh_qkv_body(x, wq, wk, wv, cos, sin, q_out, kv_out, joined, acc):
    for i, part in enumerate(chunks(x.shape[1])):
        w = jnp.concatenate([wq[part], wk[part], wv[part]], axis=1)
        joined[part] = w
        piece = jnp.dot(x[:, part], w, preferred_element_type=jnp.float32)
        acc[...] = piece if i == 0 else acc[...] + piece
    rotate(acc, cos[...], sin[...], q_out, kv_out, 0)


def fresh_qkv(x, weights, tables):
    rows, depth = x.shape
    total = sum(w.shape[1] for w in weights)
    shape = lambda *dims: jax.ShapeDtypeStruct(dims, jnp.bfloat16)
    return simple_call(
        fresh_qkv_body,
        (shape(rows, total - 2 * HEAD_WIDTH), shape(rows, 2 * HEAD_WIDTH), shape(depth, total)),
        STEP, x, *weights, *tables,
        scratch=[pltpu.VMEM((rows, total), jnp.float32)],
    )


def qkv_body(n, first, block, early, skip, *refs):
    xs, (w, table, where, *rest) = refs[:n], refs[n:]
    q_out, kv_out, acc = rest[-3:]
    for i, part in enumerate(chunks(w.shape[0])):
        x = jnp.concatenate([r[:, part] for r in xs], axis=0)
        piece = jnp.dot(x, w[part], preferred_element_type=jnp.float32)
        acc[...] = piece if i == 0 else acc[...] + piece
    base = 0
    if early:
        q_early, kv_early = rest[:2]
        base = q_early.shape[0]
        q_out[:base] = q_early[...]
        kv_out[:base] = kv_early[...]
    chips = table.shape[0] // block // 2
    spots = [start_of(where[0], chips, block, first + i) for i in range(acc.shape[0] // block)]
    spots = [pl.ds(pl.multiple_of(spot, block), block) for spot in spots]
    both = jnp.concatenate([table[spot] for spot in spots], axis=0)
    rotate(acc, both[:, :HEAD_WIDTH], both[:, HEAD_WIDTH:], q_out, kv_out, base)


def qkv(blocks, joined, table, where, first, block, cost, early=(), after=()):
    rows, (depth, total) = sum(b.shape[0] for b in blocks), joined.shape
    base = early[0].shape[0] if early else 0
    shape = lambda wide: jax.ShapeDtypeStruct((base + rows, wide), jnp.bfloat16)
    return simple_call(
        functools.partial(qkv_body, len(blocks), first, block, bool(early), len(after)),
        (shape(total - 2 * HEAD_WIDTH), shape(2 * HEAD_WIDTH)),
        cost, *blocks, joined, jnp.asarray(table), where, *early, *after,
        specs=[VMEM] * (len(blocks) + 2) + [SMEM] + [VMEM] * len(early) + [ANY] * len(after),
        scratch=[pltpu.VMEM((rows, total), jnp.float32)],
    )


def dot_t(a, b):
    return lax.dot_general(a, b, (((1,), (1,)), ((), ())), preferred_element_type=jnp.float32)


def local_body(scale, q, kv, cache_far, lengths_far, after, out, stats, cache, lengths, sems):
    copies = fetch((cache_far, lengths_far), (cache, lengths), sems)
    for copy in copies:
        copy.wait()
    width, rows = HEAD_WIDTH, q.shape[0]
    groups, samples = q.shape[1] // width, cache.shape[0]
    slots = cache.shape[1]
    query = jnp.concatenate(
        [q[:, g * width : (g + 1) * width] for g in range(groups)], axis=0
    )
    old = cache[...].reshape(samples * slots, 2 * width)
    total = groups * rows
    row = lax.broadcasted_iota(jnp.int32, (total, 1), 0) % rows
    column = lax.broadcasted_iota(jnp.int32, (1, samples * slots), 1)
    score_old = dot_t(query, old[:, :width]) * scale
    limit = row // 2 * slots + jnp.concatenate([row_lengths(lengths, rows)] * groups, axis=0)
    allowed = (column >= row // 2 * slots) & (column < limit)
    score_old = jnp.where(allowed, score_old, -jnp.inf)
    fresh = lax.broadcasted_iota(jnp.int32, (1, rows), 1)
    score_new = dot_t(query, kv[:, :width]) * scale
    score_new = jnp.where((fresh // 2 == row // 2) & (fresh <= row), score_new, -jnp.inf)
    peak = jnp.maximum(
        jnp.max(score_old, axis=1, keepdims=True), jnp.max(score_new, axis=1, keepdims=True)
    )
    expo_old, expo_new = jnp.exp(score_old - peak), jnp.exp(score_new - peak)
    both = jnp.sum(expo_old, axis=1, keepdims=True) + jnp.sum(expo_new, axis=1, keepdims=True)
    mixed = jnp.dot(
        expo_old.astype(jnp.bfloat16), old[:, width:], preferred_element_type=jnp.float32
    ) + jnp.dot(
        expo_new.astype(jnp.bfloat16), kv[:, width:], preferred_element_type=jnp.float32
    )
    out[...] = mixed
    lane = lax.broadcasted_iota(jnp.int32, stats.shape, 1)
    stats[...] = jnp.where(lane == 0, peak, both)


def local_attention(q, kv, cache, lengths, scale, after):
    total = q.shape[1] // HEAD_WIDTH * q.shape[0]
    shape = jax.ShapeDtypeStruct((total, HEAD_WIDTH), jnp.float32)
    flops = 4 * total * cache.shape[0] * cache.shape[1] * HEAD_WIDTH
    return simple_call(
        functools.partial(local_body, scale), (shape, shape), flops,
        q, kv, cache, lengths, after,
        specs=[VMEM] * 2 + [HBM] * 2 + [ANY], scratch=like(cache, lengths),
    )


def prefix_body(scale, kept, came, last, kv_a, kv_b, after, out):
    width, rows = HEAD_WIDTH, kept.shape[0]
    groups = kept.shape[1] // width
    picked = arrived(kept, came, last)
    query = jnp.concatenate([picked[:, g * width : (g + 1) * width] for g in range(groups)], axis=0)
    pairs = jnp.concatenate([kv_a[...], kv_b[...]], axis=0)
    score = dot_t(query, pairs[:, :width]) * scale
    peak = jnp.max(score, axis=1, keepdims=True)
    expo = jnp.exp(score - peak)
    both = jnp.sum(expo, axis=1, keepdims=True)
    mixed = jnp.dot(expo.astype(jnp.bfloat16), pairs[:, width:], preferred_element_type=jnp.float32)
    mixed = (mixed / both).astype(jnp.bfloat16)
    level = peak + jnp.log(both)
    lane = lax.broadcasted_iota(jnp.int32, (rows, width), 1)
    tail = jnp.zeros((rows, width), jnp.bfloat16)
    for g in range(groups):
        out[:, g * width : (g + 1) * width] = mixed[g * rows : (g + 1) * rows]
        rest = level[g * rows : (g + 1) * rows]
        for part in range(3):
            high = rest.astype(jnp.bfloat16)
            rest = rest - high.astype(jnp.float32)
            tail = jnp.where(lane == g * 3 + part, high, tail)
    out[:, groups * width :] = tail


def prefix_attention(asked, kv_a, kv_b, scale, after):
    rows, wide = asked[0].shape
    shape = jax.ShapeDtypeStruct((rows, wide + HEAD_WIDTH), jnp.bfloat16)
    return simple_call(
        functools.partial(prefix_body, scale), shape, 4 * STEP, *asked, kv_a, kv_b, after,
        specs=[VMEM] * 5 + [ANY],
    )


def merge_body(kept, came, last, local, stats, *rest):
    out = rest[-1]
    width, rows = HEAD_WIDTH, kept.shape[0]
    groups = local.shape[0] // rows
    picked = arrived(kept, came, last).astype(jnp.float32)
    tail = picked[:, groups * width :]
    for g in range(groups):
        level = tail[:, g * 3 : g * 3 + 1] + tail[:, g * 3 + 1 : g * 3 + 2]
        level = level + tail[:, g * 3 + 2 : g * 3 + 3]
        peak = stats[g * rows : (g + 1) * rows, 0:1]
        both = stats[g * rows : (g + 1) * rows, 1:2]
        top = jnp.maximum(level, peak)
        factor_pre, factor_loc = jnp.exp(level - top), jnp.exp(peak - top)
        total = factor_pre + both * factor_loc
        mixed = picked[:, g * width : (g + 1) * width] * factor_pre
        mixed = mixed + local[g * rows : (g + 1) * rows] * factor_loc
        out[:, g * width : (g + 1) * width] = (mixed / total).astype(jnp.bfloat16)


def merge(back, local, stats, after):
    rows, wide = back[0].shape
    shape = jax.ShapeDtypeStruct((rows, wide - HEAD_WIDTH), jnp.bfloat16)
    return simple_call(
        merge_body, shape, 0, *back, local, stats, *after,
        specs=[VMEM] * 5 + [ANY] * len(after),
    )


def prefill_body(scale, q_a, q_b, kv_a, kv_b, where, *rest):
    own, other = rest[-2:]
    width = HEAD_WIDTH
    groups = q_a.shape[1] // width
    block = own.shape[0] // 4
    pairs = jnp.concatenate([kv_a[...], kv_b[...]], axis=0)
    length = pairs.shape[0]

    def places(shape, axis):
        spot = lax.broadcasted_iota(jnp.int32, shape, axis)
        shift = jnp.zeros(shape, jnp.int32)
        count = length // block
        for i in range(count):
            start = start_of(where[0], count // 2, block, i)
            shift = jnp.where(spot // block == i, start - i * block, shift)
        return spot + shift

    allowed = places((length, 1), 0) >= places((1, length), 1)
    for g in range(groups):
        cols = slice(g * width, (g + 1) * width)
        query = jnp.concatenate([q_a[:, cols], q_b[:, cols]], axis=0)
        score = jnp.where(allowed, dot_t(query, pairs[:, :width]) * scale, -jnp.inf)
        expo = jnp.exp(score - jnp.max(score, axis=1, keepdims=True))
        both = jnp.sum(expo, axis=1, keepdims=True)
        mixed = jnp.dot(
            expo.astype(jnp.bfloat16), pairs[:, width:], preferred_element_type=jnp.float32
        )
        mixed = (mixed / both).astype(jnp.bfloat16)
        part = lambda i, n: mixed[i * block : (i + n) * block]
        for out, at in ((own, (0, 2, 6)), (other, (1, 4, 7))):
            out[:block, cols] = part(at[0], 1)
            out[block : 3 * block, cols] = part(at[1], 2)
            out[3 * block :, cols] = part(at[2], 1)


def prefill_attention(q_a, q_b, kv_a, kv_b, where, scale, after):
    length = q_a.shape[0] + q_b.shape[0]
    shape = jax.ShapeDtypeStruct((length // 2, q_a.shape[1]), jnp.bfloat16)
    return simple_call(
        functools.partial(prefill_body, scale),
        (shape, shape),
        4 * length * length * q_a.shape[1],
        q_a, q_b, kv_a, kv_b, where, *after,
        specs=[VMEM] * 4 + [SMEM] + [ANY] * len(after),
    )


def strips(wide):
    tile = 1024 if wide % 1024 == 0 else wide
    return [slice(i * tile, (i + 1) * tile) for i in range(wide // tile)]


def stage_body(own, other, *rest):
    both, sems = rest[-2:]
    depth = own.shape[0]
    copies = [
        pltpu.make_async_copy(own, both.at[:depth], sems.at[0]),
        pltpu.make_async_copy(other, both.at[depth:], sems.at[1]),
    ]
    for copy in copies:
        copy.start()
    for copy in copies:
        copy.wait()


def stage(own, other, after):
    shape = jax.ShapeDtypeStruct((2 * own.shape[0], own.shape[1]), own.dtype)
    return simple_call(
        stage_body, shape, 0, own, other, *after,
        specs=[HBM] * 2 + [ANY] * len(after), scratch=[pltpu.SemaphoreType.DMA((2,))],
    )


def out_body(own, other, w, *rest):
    outs = rest[1:]
    heads = jnp.concatenate([own[...], other[...]], axis=1)
    for part in strips(w.shape[1]):
        rows = jnp.dot(heads, w[:, part], preferred_element_type=jnp.float32)
        base = 0
        for out in outs:
            out[:, part] = rows[base : base + out.shape[0]].astype(out.dtype)
            base += out.shape[0]


def out_projection(own, other, w, blocks, dtype, after):
    shapes = tuple(jax.ShapeDtypeStruct((b, w.shape[1]), dtype) for b in blocks)
    return simple_call(
        out_body, shapes, 0, own, other, w, after, specs=[VMEM] * 3 + [ANY]
    )


def partial_body(tp, heads, w, kept, given):
    core = tp[0] % 2
    rows, depth = kept.shape[0], heads.shape[1]
    for columns in strips(w.shape[1]):
        part = jnp.dot(heads[...], w[:depth, columns], preferred_element_type=jnp.float32)
        low, high = part[:rows], part[rows:]
        kept[:, columns] = jnp.where(core == 0, low, high).astype(kept.dtype)
        given[:, columns] = jnp.where(core == 0, high, low).astype(given.dtype)


def partial_projection(tp, heads, w):
    shape = jax.ShapeDtypeStruct((heads.shape[0] // 2, w.shape[1]), jnp.bfloat16)
    return simple_call(
        partial_body, (shape, shape), TAIL, tp, heads, w, specs=[SMEM, VMEM, VMEM]
    )


def add_body(a, b, *rest):
    out = rest[-1]
    out[...] = (a[...].astype(jnp.float32) + b[...].astype(jnp.float32)).astype(out.dtype)


def add(a, b, dtype, after=()):
    shape = jax.ShapeDtypeStruct(a.shape, dtype)
    specs = [VMEM] * 2 + [ANY] * len(after)
    return simple_call(add_body, shape, TAIL, a, b, *after, specs=specs)


def add_four_body(own, far, down, up, *rest):
    out = rest[-1]
    wide = own[...].astype(jnp.float32) + far[...].astype(jnp.float32)
    out[...] = wide + (down[...].astype(jnp.float32) + up[...].astype(jnp.float32))


def add_four(own, far, down, up, after):
    shape = jax.ShapeDtypeStruct(own.shape, jnp.float32)
    specs = [VMEM] * 4 + [ANY] * len(after)
    return simple_call(add_four_body, shape, TAIL, own, far, down, up, *after, specs=specs)


def add_half_body(first, whole, part, *rest):
    out = rest[-1]
    half = part.shape[0]
    for i in range(2):
        rows = slice(i * half, (i + 1) * half)
        if i == first:
            wide = whole[rows].astype(jnp.float32) + part[...].astype(jnp.float32)
            out[rows] = wide.astype(out.dtype)
        else:
            out[rows] = whole[rows]


def add_half(first, whole, part, after):
    shape = jax.ShapeDtypeStruct(whole.shape, whole.dtype)
    specs = [VMEM] * 2 + [ANY] * len(after)
    body = functools.partial(add_half_body, first)
    return simple_call(body, shape, 0, whole, part, *after, specs=specs)


def total_body(a, b, c, d, out, token):
    token[...] = jnp.zeros(token.shape, token.dtype)
    wide = a[...].astype(jnp.float32) + b[...].astype(jnp.float32)
    wide = wide + (c[...].astype(jnp.float32) + d[...].astype(jnp.float32))
    out[...] = wide.astype(out.dtype)


def finish_body(tp, kept, taken, tokens, out):
    core = tp[0] % 2
    for i in range(out.shape[0]):
        row = 2 * i % kept.shape[0]
        first = i < out.shape[0] // 2
        held, sent = kept[row : row + 2], taken[row : row + 2]
        total = jnp.where(core == 0, held if first else sent, sent if first else held)
        out[i] = tokens[i].astype(jnp.float32) + total


def finish(tp, kept, taken, tokens):
    shape = jax.ShapeDtypeStruct(tokens.shape, jnp.float32)
    return simple_call(
        finish_body, shape, TAIL, tp, kept, taken, tokens,
        specs=[SMEM] + [VMEM] * 3,
    )


def shards(
    prompt_states,
    new_states,
    answer_cache,
    attn_gain,
    w_query,
    key_weight,
    value_weight,
    w_out,
    prompt_of,
    suffix_len,
):
    scale = HEAD_WIDTH ** (-0.5)
    rows = prompt_states[0, 0]
    block, width = rows.shape
    tp, grp = lax.axis_index("tp").reshape(1), lax.axis_index("grp").reshape(1)
    tp_size = lax.axis_size("tp")

    def around(value, by):
        return lax.ppermute(value, "tp", [(i, (i + 2 * by) % tp_size) for i in range(tp_size)])

    def swap(value, axis, mask):
        return lax.ppermute(value, axis, [(i, i ^ mask) for i in range(lax.axis_size(axis))])

    weights = (w_query, key_weight, value_weight)
    half = block // 2

    normed = norm_prompt(rows, attn_gain, tp, grp)
    from_down = around(normed, 1)
    from_up = around(normed, -1)
    mate_own = swap(normed, "tp", 1)

    samples, slots = new_states.shape[1], answer_cache.shape[2]
    length = block * tp_size
    fresh_normed, *fresh_tables, forth, home = prepare_fresh(
        grp, new_states[0], attn_gain, suffix_len, fixed_tables(length, slots + 8), prompt_of
    )
    fresh_q, fresh_kv, weights = fresh_qkv(fresh_normed, weights, fresh_tables)
    w_mate = swap(w_out, "tp", 1)

    where = tp
    tables = fixed_tables(0, length)
    asked = exchange_near(fresh_q, swap, ())
    early = qkv([normed, mate_own], weights, tables, where, 0, block, STEP)
    kept, third, fourth = exchange_pick(asked, forth, swap, ())
    from_down, from_up = hold((from_down, from_up), (third, early[1]))
    down_top, up_low = cut(from_down, from_up)
    ahead = around(down_top, 1)
    behind = around(up_low, -1)
    near = [from_down, from_up, swap(from_down, "tp", 1), swap(from_up, "tp", 1)]
    q_a, kv_a = qkv(near, weights, tables, where, 2, block, 0, early)
    handed_a = swap(kv_a, "role", 1)
    w_both = stage(w_out, w_mate, (kv_a,))
    local, stats = local_attention(fresh_q, fresh_kv, answer_cache[0], suffix_len, scale, w_both)
    came, fourth = exchange_pass(third, fourth, swap, ())
    ahead, behind = hold((ahead, behind), (local,))
    last = swap(fourth, "grp", FOURTH)
    far = [ahead, behind, swap(ahead, "tp", 1), swap(behind, "tp", 1)]
    q_b, kv_b = qkv(far, weights, tables, where, 6, block, 0)
    handed_b = swap(kv_b, "role", 1)

    heads_own, heads_other = prefill_attention(q_a, q_b, kv_a, kv_b, where, scale, ())
    heads_mate = swap(heads_other, "tp", 1)

    asked = (kept, came, last)
    answered = prefix_attention(asked, handed_a, handed_b, scale, heads_own)

    sizes = (block, block, block, half, half)
    to_own, to_down, to_up, far_top, far_low = out_projection(
        heads_own, heads_mate, w_both, sizes, jnp.bfloat16, answered
    )
    via_up = around(far_top, 1)
    via_down = around(far_low, -1)

    back = exchange_near(answered, swap, (), STEP)
    kept, third, fourth = exchange_pick(back, home, swap, (), STEP)
    up = add_half(0, to_up, via_up, (third,))
    down = add_half(1, to_down, via_down, (third,))
    came, fourth = exchange_pass(third, fourth, swap, (up, down), STEP)
    back = (kept, came, swap(fourth, "grp", FOURTH))
    sum_up = around(up, 1)
    sum_down = around(down, -1)
    prefill_out, token = simple_call(
        total_body,
        (jax.ShapeDtypeStruct(rows.shape, rows.dtype), jax.ShapeDtypeStruct((8, 128), jnp.float32)),
        0, rows, to_own, sum_up, sum_down,
    )

    decoded = merge(back, local, stats, (up, down))
    kept, given = partial_projection(tp, decoded, w_both)
    level = add(kept, swap(given, "tp", 1), jnp.bfloat16)
    summed = add_four(level, around(level, 2), around(level, 1), around(level, -1), (token,))
    decode_out = finish(tp, summed, swap(summed, "tp", 1), new_states[0])
    return prefill_out[None, None], decode_out[None]


def solution(mesh):
    placed = (
        P("role", "grp", "tp", None),
        P("role", "grp", None, None),
        P("role", "grp", None, "tp"),
        P(),
        P(None, "tp"),
        P(None, "tp"),
        P(None, "tp"),
        P("tp", None),
        P("role", None),
        P("role", "grp"),
    )
    return jax.shard_map(
        shards,
        mesh=mesh,
        in_specs=placed,
        out_specs=(P("role", "grp", "tp", None), P("role", "grp", None, None)),
        check_vma=False,
    )
```
